256 devices in a mesh: wide: 32 (over x, y, core), narrow: 8 (over z).
Axes of the slice: x: 4, y: 4, z: 8, core: 2. Of those that a mesh axis runs over, the one named last changes fastest.
Arguments:
- tokens: bfloat16 [16384, 4096], P('wide', 'narrow'), may hold values from -40 to 40
- norm_gain: float32 [4096], P('narrow'), may hold values from 0.5 to 5
- w_query: bfloat16 [4096, 4096], P(None, 'narrow'), may hold values from -0.09375 to 0.09375
- key_weight: bfloat16 [4096, 1024], P(None, 'narrow'), may hold values from -0.09375 to 0.09375
- value_weight: bfloat16 [4096, 1024], P(None, 'narrow'), may hold values from -0.09375 to 0.09375
- w_out: bfloat16 [4096, 4096], P('narrow'), may hold values from -0.09375 to 0.09375
- doc_lengths: int32 [64], replicated, may hold values from 1 to 8192, 16384 in all
Outputs:
- attended: bfloat16 [16384, 4096], P('wide', 'narrow')
The draws below stay inside these ranges and needn't reach their ends.
Inputs may be any that keep to these rules, and one draw needn't show every extreme that they name: `doc_lengths`: the lengths sum to 16384; the longest is exactly 8192.
All inputs are finite; a program needn't handle non-finite values.
Results may differ from the reference program's by a relative error of at most 0.019.
The reference program's roundings to bfloat16 on the way count: a program that leaves them out, or rounds other values in their place, can miss the bound.
Values may be sent and summed in bfloat16 or wider, within the bound.
No kernel may reach another device: no remote copies, remote signals or barrier semaphores. Data moves between devices by JAX's collectives and lax.ppermute only.
A program may use at most 128 MiB of HBM per device.

```python
import math
import jax
import jax.numpy as jnp
import numpy as np
from jax import lax

MODEL_WIDTH = 4096
QUERY_HEADS = 32
KEY_VALUE_HEADS = 8
HEAD_SIZE = 128
PACKED_TOKENS = 16384
LONGEST_DOC = 8192
DOCS = 64
N_NARROW = 8


def draw_tokens(key, part):
    key = jax.random.fold_in(key, 11)
    column_scale = 0.5 + jnp.arange(MODEL_WIDTH, dtype=jnp.float32) / MODEL_WIDTH
    values = jnp.clip(jax.random.normal(key, (PACKED_TOKENS, MODEL_WIDTH), jnp.float32), -6.0, 6.0) * column_scale[None, :]
    return values.astype(jnp.bfloat16)


def draw_norm_gain(key, part):
    key = jax.random.fold_in(key, 23)
    values = jax.random.uniform(key, (MODEL_WIDTH,), jnp.float32, 0.5, 1.5)
    return values


def shard_levels(own_key, dims, cuts, least, largest):
    level = 1.0
    for axis_at, blocks in cuts:
        heights = jax.random.uniform(jax.random.fold_in(jax.random.fold_in(own_key, 6), axis_at), (blocks,), jnp.float32, least / len(cuts), largest / len(cuts))
        level = level * jnp.repeat(jnp.exp(heights), dims[axis_at] // blocks).reshape((-1,) + (1,) * (len(dims) - 1 - axis_at))
    return level


def profile(amount, total, reach, skew):
    portions = [(1 << 20) // math.isqrt(rank ** skew) + 1 for rank in range(2, amount + 1)]
    rest, holding = total - reach - (amount - 1), [1] * (amount - 1)
    while rest > 0:
        movable = [i for i in range(amount - 1) if holding[i] < reach]
        whole, left = sum([portions[i] for i in movable]), rest
        for i in movable:
            addition = min(reach - holding[i], max(1, left * portions[i] // whole), rest)
            holding[i] = holding[i] + addition
            rest = rest - addition
    return np.array([reach] + holding)


def uneven(own_key, number_of, total, limit, slope):
    if number_of == 2:
        one = jax.random.randint(own_key, (), max(1, total - limit), min(limit, total - 1) + 1)
        return jnp.stack([one, total - one])
    tallies = jnp.asarray(profile(number_of, total, limit, slope), jnp.int32)
    couples = (number_of - 1) // 2
    giver, taker = tallies[1:1 + 2 * couples:2], tallies[2:2 + 2 * couples:2]
    margin = jnp.minimum(giver - 1, limit - taker)
    passed = jax.random.randint(jax.random.fold_in(own_key, 1), (couples,), 0, 1 << 20) % (margin + 1)
    tallies = tallies.at[1:1 + 2 * couples:2].set(giver - passed).at[2:2 + 2 * couples:2].set(taker + passed)
    return tallies[jax.random.permutation(jax.random.fold_in(own_key, 2), number_of)]


def scatter_about(key, extent, deviation, most, pieces=(), kind=jnp.bfloat16):
    array = deviation * jax.random.normal(key, extent, jnp.float32)
    if pieces:
        array = array * shard_levels(key, extent, pieces, -0.22, 0.18)
    return jnp.clip(array, -most, most).astype(kind)


def setup_inputs(seed: int = 0) -> dict:
    arg_keys = jax.random.split(jax.random.key(seed), 8)
    return {
        "tokens": draw_tokens(jax.random.fold_in(arg_keys[7], 71), 0),
        "norm_gain": draw_norm_gain(jax.random.fold_in(arg_keys[7], 71), 0),
        "w_query": scatter_about(arg_keys[2], (MODEL_WIDTH, QUERY_HEADS * HEAD_SIZE), MODEL_WIDTH ** -0.5, 0.09375, ((1, 8),)),
        "key_weight": scatter_about(arg_keys[3], (MODEL_WIDTH, KEY_VALUE_HEADS * HEAD_SIZE), MODEL_WIDTH ** -0.5, 0.09375, ((1, 8),)),
        "value_weight": scatter_about(arg_keys[4], (MODEL_WIDTH, KEY_VALUE_HEADS * HEAD_SIZE), MODEL_WIDTH ** -0.5, 0.09375, ((1, 8),)),
        "w_out": scatter_about(arg_keys[5], (QUERY_HEADS * HEAD_SIZE, MODEL_WIDTH), (QUERY_HEADS * HEAD_SIZE) ** -0.5, 0.09375, ((0, 8),)),
        "doc_lengths": uneven(arg_keys[6], DOCS, PACKED_TOKENS, LONGEST_DOC, 2).astype(jnp.int32),
    }


EPSILON = 1e-05
ROPE_BASE = 500000.0
NEGATIVE = -1e+30

def doc_of(lengths, positions):
    starts = (jnp.cumsum(lengths) - lengths).astype(jnp.int32)
    return (lax.optimization_barrier(jnp.sum((starts[None, :] <= positions[:, None]).astype(jnp.int32), axis=1)) - 1).astype(jnp.int32)

def doc_info(lengths, positions):
    starts = (jnp.cumsum(lengths) - lengths).astype(jnp.int32)
    docs = doc_of(lengths, positions)
    onehot = docs[:, None] == jnp.arange(lengths.shape[0], dtype=jnp.int32)[None, :]
    first_tok = lax.optimization_barrier(jnp.sum(jnp.where(onehot, starts[None, :], 0), axis=1)).astype(jnp.int32)
    return (docs, (positions - first_tok).astype(jnp.int32))

def apply_rotary(values, rotary_positions):
    half_width = values.shape[-1] // 2
    frequency = ROPE_BASE ** (-(jnp.arange(half_width, dtype=jnp.float32) * 2.0 / values.shape[-1]))
    angles = rotary_positions.astype(jnp.float32)[:, None] * frequency[None, :]
    cosine = jnp.cos(angles)[:, None, :]
    sine_part = jnp.sin(angles)[:, None, :]
    first_half = values[..., :half_width]
    second_half = values[..., half_width:]
    return jnp.concatenate([first_half * cosine - second_half * sine_part, second_half * cosine + first_half * sine_part], axis=-1)

def reference(tokens, norm_gain, w_query, key_weight, value_weight, w_out, doc_lengths):
    as_float = tokens.astype(jnp.float32)
    inverse = lax.rsqrt(lax.optimization_barrier(jnp.sum(as_float * as_float, axis=1, keepdims=True)) / MODEL_WIDTH + EPSILON)
    normed = (as_float * inverse * norm_gain[None, :]).astype(jnp.bfloat16)
    query_raw = jnp.dot(normed, w_query, preferred_element_type=jnp.float32)
    key_unrotated = jnp.dot(normed, key_weight, preferred_element_type=jnp.float32)
    value_projected = jnp.dot(normed, value_weight, preferred_element_type=jnp.float32)
    positions = jnp.arange(PACKED_TOKENS, dtype=jnp.int32)
    docs, rotary_positions = doc_info(doc_lengths, positions)
    query_rows = apply_rotary(query_raw.reshape(PACKED_TOKENS, QUERY_HEADS, HEAD_SIZE), rotary_positions).astype(jnp.bfloat16)
    rotated_keys = apply_rotary(key_unrotated.reshape(PACKED_TOKENS, KEY_VALUE_HEADS, HEAD_SIZE), rotary_positions).astype(jnp.bfloat16)
    every_value = value_projected.reshape(PACKED_TOKENS, KEY_VALUE_HEADS, HEAD_SIZE).astype(jnp.bfloat16)
    heads_per_group = QUERY_HEADS // KEY_VALUE_HEADS
    rows_per_block = math.gcd(PACKED_TOKENS, 512)
    key_window = LONGEST_DOC + rows_per_block
    score_scale = 1.0 / math.sqrt(HEAD_SIZE)
    padded_keys = jnp.concatenate([jnp.zeros((LONGEST_DOC, KEY_VALUE_HEADS, HEAD_SIZE), jnp.bfloat16), rotated_keys], axis=0)
    padded_values = jnp.concatenate([jnp.zeros((LONGEST_DOC, KEY_VALUE_HEADS, HEAD_SIZE), jnp.bfloat16), every_value], axis=0)
    docs_padded = jnp.concatenate([-jnp.ones((LONGEST_DOC,), jnp.int32), docs], axis=0)
    pos_padded = (jnp.arange(PACKED_TOKENS + LONGEST_DOC, dtype=jnp.int32) - LONGEST_DOC).astype(jnp.int32)

    def one_block(block_index):
        first_row = (block_index * rows_per_block).astype(jnp.int32)
        block_of_queries = lax.dynamic_slice_in_dim(query_rows, first_row, rows_per_block, 0).reshape(rows_per_block, KEY_VALUE_HEADS, heads_per_group, HEAD_SIZE)
        query_doc = lax.dynamic_slice_in_dim(docs, first_row, rows_per_block, 0)
        query_pos = first_row + jnp.arange(rows_per_block, dtype=jnp.int32)
        key_tile = lax.dynamic_slice_in_dim(padded_keys, first_row, key_window, 0)
        value_tile = lax.dynamic_slice_in_dim(padded_values, first_row, key_window, 0)
        key_doc = lax.dynamic_slice_in_dim(docs_padded, first_row, key_window, 0)
        key_pos = lax.dynamic_slice_in_dim(pos_padded, first_row, key_window, 0)
        allowed = (key_doc[None, :] == query_doc[:, None]) & (key_pos[None, :] <= query_pos[:, None])

        def one_head(operands):
            query_head, key_head, value_head = operands
            scores = jnp.einsum('rgd,nd->grn', query_head.astype(jnp.float32), key_head.astype(jnp.float32)) * score_scale
            masked = jnp.where(allowed[None], scores, NEGATIVE)
            row_max = lax.optimization_barrier(jnp.max(masked, axis=-1, keepdims=True))
            weights = jnp.where(allowed[None], jnp.exp(scores - row_max), 0.0)
            row_total = lax.optimization_barrier(jnp.sum(weights, axis=-1))
            rounded = lax.optimization_barrier(weights.astype(jnp.bfloat16)).astype(jnp.float32)
            mixed = jnp.einsum('grn,nd->grd', rounded, value_head.astype(jnp.float32)) / row_total[..., None]
            return mixed.astype(jnp.bfloat16)
        head_out = lax.map(one_head, (block_of_queries.transpose(1, 0, 2, 3), key_tile.transpose(1, 0, 2), value_tile.transpose(1, 0, 2)))
        return head_out.transpose(2, 0, 1, 3).reshape(rows_per_block, QUERY_HEADS * HEAD_SIZE)
    heads_all = lax.map(one_block, jnp.arange(PACKED_TOKENS // rows_per_block, dtype=jnp.int32)).reshape(PACKED_TOKENS, QUERY_HEADS * HEAD_SIZE)
    group_cols = QUERY_HEADS * HEAD_SIZE // N_NARROW
    summed = jnp.zeros((PACKED_TOKENS, MODEL_WIDTH), jnp.float32)
    for group_index in range(N_NARROW):
        lower = group_index * group_cols
        product = jnp.dot(heads_all[:, lower:lower + group_cols], w_out[lower:lower + group_cols], preferred_element_type=jnp.float32)
        summed = summed + lax.optimization_barrier(product.astype(jnp.bfloat16)).astype(jnp.float32)
    return summed.astype(jnp.bfloat16)
```

```python
import functools
import math

import jax
import jax.numpy as jnp
from jax import lax
from jax.experimental import pallas as pl
from jax.experimental.pallas import tpu as pltpu
from jax.sharding import PartitionSpec as P

MODEL_WIDTH = 4096
HEAD_SIZE = 128
EPSILON = 1e-05
ROPE_BASE = 500000.0
NEGATIVE = -1e30
VMEM_LIMIT = 56 * 1024 * 1024

_NT = (((1,), (1,)), ((), ()))


def project_kernel(x_ref, gain_ref, w_ref, cos_ref, sin_ref, q_ref, k_ref, vt_ref):
    x = x_ref[...].astype(jnp.float32)
    squares = jnp.sum(x * x, axis=1, keepdims=True)
    inverse = lax.rsqrt(squares / MODEL_WIDTH + EPSILON)
    normed = (x * inverse * gain_ref[...]).astype(jnp.bfloat16)
    raw = jnp.dot(normed, w_ref[...], preferred_element_type=jnp.float32)
    cos, sin = cos_ref[...], sin_ref[...]
    heads = q_ref.shape[0]
    for h in range(heads + 1):
        part = raw[:, h * HEAD_SIZE : (h + 1) * HEAD_SIZE]
        turned = (part * cos + pltpu.roll(part, HEAD_SIZE // 2, 1) * sin).astype(jnp.bfloat16)
        if h < heads:
            q_ref[h] = turned
        else:
            k_ref[...] = turned
    vt_ref[...] = raw[:, (heads + 1) * HEAD_SIZE :].T.astype(jnp.bfloat16)


def project(x, gain, weights, cos, sin, heads):
    rows = x.shape[0]
    block = math.gcd(rows, 128)
    width = weights.shape[1]
    return pl.pallas_call(
        project_kernel,
        grid=(rows // block,),
        in_specs=[
            pl.BlockSpec((block, MODEL_WIDTH), lambda i: (i, 0)),
            pl.BlockSpec((1, MODEL_WIDTH), lambda i: (0, 0)),
            pl.BlockSpec((MODEL_WIDTH, width), lambda i: (0, 0)),
            pl.BlockSpec((block, HEAD_SIZE), lambda i: (i, 0)),
            pl.BlockSpec((block, HEAD_SIZE), lambda i: (i, 0)),
        ],
        out_specs=[
            pl.BlockSpec((heads, block, HEAD_SIZE), lambda i: (0, i, 0)),
            pl.BlockSpec((block, HEAD_SIZE), lambda i: (i, 0)),
            pl.BlockSpec((HEAD_SIZE, block), lambda i: (0, i)),
        ],
        out_shape=[
            jax.ShapeDtypeStruct((heads, rows, HEAD_SIZE), jnp.bfloat16),
            jax.ShapeDtypeStruct((rows, HEAD_SIZE), jnp.bfloat16),
            jax.ShapeDtypeStruct((HEAD_SIZE, rows), jnp.bfloat16),
        ],
        compiler_params=pltpu.CompilerParams(vmem_limit_bytes=VMEM_LIMIT),
        cost_estimate=pl.CostEstimate(
            flops=2 * rows * MODEL_WIDTH * width,
            bytes_accessed=2 * (rows * MODEL_WIDTH + MODEL_WIDTH * width),
            transcendentals=0,
        ),
        name="norm_project",
    )(x, gain, weights, cos, sin)


def attend_kernel(
    tile, info_ref, first_ref, q_ref, k_hbm, vt_hbm, w_hbm, out_hbm,
    k_buf, v_buf, w_buf, out_buf, top_ref, total_ref, mix_ref, k_sem, v_sem, w_sem, out_sem,
):
    low, own, base, late = info_ref[0], info_ref[1], info_ref[2], info_ref[3]
    heads, rows = q_ref.shape[0], q_ref.shape[1]
    factor = math.log2(math.e) / math.sqrt(HEAD_SIZE)

    def key_copy(j):
        return pltpu.make_async_copy(k_hbm.at[j], k_buf.at[j], k_sem.at[j])

    def value_copy(j):
        return pltpu.make_async_copy(vt_hbm.at[j], v_buf.at[j], v_sem.at[j])

    def start(j):
        key_copy(j).start()
        value_copy(j).start()

    start(own)
    lax.fori_loop(low, own, lambda j, _: (start(j), 0)[1], 0)
    w_copy = pltpu.make_async_copy(w_hbm, w_buf, w_sem)
    w_copy.start()

    top_ref[...] = jnp.full(top_ref.shape, NEGATIVE, jnp.float32)
    total_ref[...] = jnp.zeros(total_ref.shape, jnp.float32)
    mix_ref[...] = jnp.zeros(mix_ref.shape, jnp.float32)

    def step(j, masked):
        keys, values = k_buf[j], v_buf[j]
        if masked:
            key_pos = j * tile + lax.broadcasted_iota(jnp.int32, (tile, rows), 0)
            query_pos = base + lax.broadcasted_iota(jnp.int32, (tile, rows), 1)
            allowed = (key_pos >= first_ref[...]) & (key_pos <= query_pos)
        for h in range(heads):
            scores = lax.dot_general(keys, q_ref[h], _NT, preferred_element_type=jnp.float32)
            if masked:
                scores = jnp.where(allowed, scores, NEGATIVE)
            old = top_ref[h]
            new = jnp.maximum(old, jnp.max(scores, axis=0, keepdims=True))
            weights = jnp.exp2(scores * factor - new * factor)
            shrink = jnp.exp2((old - new) * factor)
            top_ref[h] = new
            total_ref[h] = total_ref[h] * shrink + jnp.sum(weights, axis=0, keepdims=True)
            mix_ref[h] = mix_ref[h] * shrink + jnp.dot(
                values, weights.astype(jnp.bfloat16), preferred_element_type=jnp.float32
            )

    def visit(j):
        key_copy(j).wait()
        value_copy(j).wait()
        clear = (j * tile >= late) & (j * tile + tile - 1 <= base)

        @pl.when(clear)
        def _():
            step(j, False)

        @pl.when(jnp.logical_not(clear))
        def _():
            step(j, True)

    visit(own)
    lax.fori_loop(low, own, lambda j, _: (visit(j), 0)[1], 0)

    mixed = jnp.concatenate(
        [(mix_ref[h] / total_ref[h]).T.astype(jnp.bfloat16) for h in range(heads)], axis=1
    )
    w_copy.wait()
    count = out_sem.shape[0]
    width = out_buf.shape[1] // count
    copies = []
    for n in range(count):
        columns = pl.ds(n * width, width)
        out_buf[:, columns] = jnp.dot(
            mixed, w_buf[:, columns], preferred_element_type=jnp.float32
        ).astype(jnp.bfloat16)
        copy = pltpu.make_async_copy(out_buf.at[:, columns], out_hbm.at[:, columns], out_sem.at[n])
        copy.start()
        copies.append(copy)
    for copy in copies:
        copy.wait()


def attend(info, first, q, keys, values, w_out):
    heads, rows, _ = q.shape
    tiles, tile, _ = keys.shape
    width = w_out.shape[1]
    anywhere = pl.BlockSpec(memory_space=pl.ANY)
    vmem = pl.BlockSpec(memory_space=pltpu.VMEM)
    return pl.pallas_call(
        functools.partial(attend_kernel, tile),
        in_specs=[pl.BlockSpec(memory_space=pltpu.SMEM), vmem, vmem, anywhere, anywhere, anywhere],
        out_specs=anywhere,
        out_shape=jax.ShapeDtypeStruct((rows, width), jnp.bfloat16),
        scratch_shapes=[
            pltpu.VMEM(keys.shape, jnp.bfloat16),
            pltpu.VMEM(values.shape, jnp.bfloat16),
            pltpu.VMEM(w_out.shape, jnp.bfloat16),
            pltpu.VMEM((rows, width), jnp.bfloat16),
            pltpu.VMEM((heads, 1, rows), jnp.float32),
            pltpu.VMEM((heads, 1, rows), jnp.float32),
            pltpu.VMEM((heads, HEAD_SIZE, rows), jnp.float32),
            pltpu.SemaphoreType.DMA((tiles,)),
            pltpu.SemaphoreType.DMA((tiles,)),
            pltpu.SemaphoreType.DMA,
            pltpu.SemaphoreType.DMA((4,)),
        ],
        compiler_params=pltpu.CompilerParams(vmem_limit_bytes=VMEM_LIMIT),
        cost_estimate=pl.CostEstimate(
            flops=4 * heads * rows * HEAD_SIZE * tiles * tile // 2,
            bytes_accessed=2 * (keys.size + values.size + w_out.size),
            transcendentals=heads * rows * tiles * tile // 2,
        ),
        name="attend",
    )(info, first, q, keys, values, w_out)


def per_device(tokens, norm_gain, w_query, key_weight, value_weight, w_out, doc_lengths):
    rows = tokens.shape[0]
    wide_index = lax.axis_index("wide")
    heads = w_query.shape[1] // HEAD_SIZE

    full = lax.all_gather(tokens, "narrow", axis=1, tiled=True)
    gain = lax.all_gather(norm_gain, "narrow", axis=0, tiled=True)
    weights = jnp.concatenate([w_query, key_weight, value_weight], axis=1)

    with jax.named_scope("positions"):
        docs = doc_lengths.shape[0]
        earlier = jnp.arange(docs)[None, :] < jnp.arange(docs)[:, None]
        starts = jnp.sum(jnp.where(earlier, doc_lengths[None, :], 0), axis=1)
        base = wide_index * rows
        positions = base + jnp.arange(rows, dtype=jnp.int32)
        first = jnp.max(
            jnp.where(starts[None, :] <= positions[:, None], starts[None, :], 0), axis=1
        ).astype(jnp.int32)
        half = HEAD_SIZE // 2
        frequency = ROPE_BASE ** (-(jnp.arange(half, dtype=jnp.float32) * 2.0 / HEAD_SIZE))
        angles = (positions - first).astype(jnp.float32)[:, None] * frequency[None, :]
        cosine, sine = jnp.cos(angles), jnp.sin(angles)
        cos = jnp.concatenate([cosine, cosine], axis=1)
        sin = jnp.concatenate([-sine, sine], axis=1)
        info = jnp.stack([first[0] // rows, wide_index, base, first[-1]]).astype(jnp.int32)

    q, k, vt = project(full, gain.reshape(1, -1), weights, cos, sin, heads)
    keys = lax.all_gather(k, "wide", axis=0)
    values = lax.all_gather(vt, "wide", axis=0)
    partial_out = attend(info, first.reshape(1, -1), q, keys, values, w_out)
    return lax.psum_scatter(partial_out, "narrow", scatter_dimension=1, tiled=True)


def solution(mesh):
    in_specs = (
        P("wide", "narrow"),
        P("narrow"),
        P(None, "narrow"),
        P(None, "narrow"),
        P(None, "narrow"),
        P("narrow", None),
        P(),
    )
    return jax.shard_map(
        per_device, mesh=mesh, in_specs=in_specs, out_specs=P("wide", "narrow"), check_vma=False
    )
```

```python
import functools
import math

import jax
import jax.numpy as jnp
from jax import lax
from jax.experimental import pallas as pl
from jax.experimental.pallas import tpu as pltpu
from jax.sharding import PartitionSpec as P

MODEL_WIDTH = 4096
HEAD_SIZE = 128
EPSILON = 1e-05
ROPE_BASE = 500000.0
NEGATIVE = -1e30
PROJECT_VMEM = 48 * 1024 * 1024
ATTEND_VMEM = 52 * 1024 * 1024
PARTS = 2
GROUPS = 2
SIDE_X, SIDE_Y, CORES = 4, 4, 2
AWAY = (0, 2, 1, -1)
SPAN = 512

_NT = (((1,), (1,)), ((), ()))
VMEM = pl.BlockSpec(memory_space=pltpu.VMEM)
SMEM = pl.BlockSpec(memory_space=pltpu.SMEM)
ANYWHERE = pl.BlockSpec(memory_space=pl.ANY)


def ring_pairs(count, index_of):
    up = [(i, index_of(i, 1)) for i in range(count)]
    return up, [(b, a) for a, b in up]


def shift_x(i, by):
    line = SIDE_Y * CORES
    return (i // line + by) % SIDE_X * line + i % line


def shift_y(i, by):
    line = SIDE_Y * CORES
    y = (i // CORES % SIDE_Y + by) % SIDE_Y
    return i // line * line + y * CORES + i % CORES


def shift_yc(i, by):
    line = SIDE_Y * CORES
    return i // line * line + (i % line + by) % line


def shift_xc(i, by):
    line = SIDE_Y * CORES
    at = (i // line * CORES + i % CORES + by) % (SIDE_X * CORES)
    return at // CORES * line + i % line // CORES * CORES + at % CORES


def ring_gather(x, axis, up, down, count):
    below, above = [], []
    for _ in range(count // 2 - 1):
        below.append(lax.ppermute(below[-1] if below else x, axis, up))
        above.append(lax.ppermute(above[-1] if above else x, axis, down))
    half = x.shape[0] // 2
    far = lax.ppermute(below[-1][:half], axis, up), lax.ppermute(above[-1][half:], axis, down)
    return below, above, far


def project_kernel(
    part, z_ref, own, b1, b2, b3, a1, a2, a3, far_b, far_a, gain_ref, wq_hbm, wk_hbm, wv_hbm, cos_ref, sin_ref,
    q_ref, k_ref, vt_ref, normed_ref, wq_ref, wk_ref, wv_ref, sem,
):
    copies = [
        pltpu.make_async_copy(hbm, ref, sem.at[i])
        for i, (hbm, ref) in enumerate(((wq_hbm, wq_ref), (wk_hbm, wk_ref), (wv_hbm, wv_ref)))
    ]
    for copy in copies:
        copy.start()
    z = z_ref[0]
    narrow = 8
    width = own.shape[1]
    rows, half = own.shape[0], own.shape[0] // 2
    pieces = [(0, own), (1, b1), (2, b2), (3, b3), (-1, a1), (-2, a2), (-3, a3)]
    heads = q_ref.shape[1] // half
    for at in range(GROUPS):
        here = slice(at * half, (at + 1) * half)
        far = (far_b, far_a)[at]
        views = [(k, ref, here) for k, ref in pieces] + [(4, far, slice(0, half))]
        squares = jnp.zeros((half, 1), jnp.float32)
        for _, ref, span in views:
            x = ref[span, :].astype(jnp.float32)
            squares = squares + jnp.sum(x * x, axis=1, keepdims=True)
        inverse = lax.rsqrt(squares / MODEL_WIDTH + EPSILON)
        for k, ref, span in views:
            source = lax.rem(z - k + narrow, narrow)
            columns = pl.ds(pl.multiple_of(source * width, width), width)
            x = ref[span, :].astype(jnp.float32)
            normed_ref[here, columns] = (x * inverse * gain_ref[:, columns]).astype(jnp.bfloat16)
        if at == 0:
            for copy in copies:
                copy.wait()
        raw_q, raw_k, raw_v = (
            jnp.dot(normed_ref[here, :], ref[...], preferred_element_type=jnp.float32)
            for ref in (wq_ref, wk_ref, wv_ref)
        )
        turn = slice(part * rows + at * half, part * rows + (at + 1) * half)
        cos, sin = cos_ref[turn, :], sin_ref[turn, :]
        for h in range(heads + 1):
            head = raw_q[:, h * HEAD_SIZE : (h + 1) * HEAD_SIZE] if h < heads else raw_k
            turned = head * cos + pltpu.roll(head, HEAD_SIZE // 2, 1) * sin
            if h < heads:
                q_ref[at, h * half : (h + 1) * half, :] = turned.astype(jnp.bfloat16)
            else:
                k_ref[here, :] = turned.astype(jnp.bfloat16)
        vt_ref[at * HEAD_SIZE : (at + 1) * HEAD_SIZE, :] = raw_v.T.astype(jnp.bfloat16)


def project(part, z, own, gathered, gain, weights, cos, sin, heads):
    below, above, far = gathered
    rows, width = own.shape[0], sum(w.shape[1] for w in weights)
    return pl.pallas_call(
        functools.partial(project_kernel, part),
        in_specs=[SMEM] + [VMEM] * 10 + [ANYWHERE] * 3 + [VMEM] * 2,
        out_specs=[VMEM] * 3,
        out_shape=[
            jax.ShapeDtypeStruct((GROUPS, heads * (rows // GROUPS), HEAD_SIZE), jnp.bfloat16),
            jax.ShapeDtypeStruct((rows, HEAD_SIZE), jnp.bfloat16),
            jax.ShapeDtypeStruct((GROUPS * HEAD_SIZE, rows // GROUPS), jnp.bfloat16),
        ],
        scratch_shapes=[pltpu.VMEM((rows, MODEL_WIDTH), jnp.bfloat16)]
        + [pltpu.VMEM(w.shape, jnp.bfloat16) for w in weights]
        + [pltpu.SemaphoreType.DMA((3,))],
        compiler_params=pltpu.CompilerParams(vmem_limit_bytes=PROJECT_VMEM),
        cost_estimate=pl.CostEstimate(
            flops=2 * rows * MODEL_WIDTH * width,
            bytes_accessed=2 * (rows * MODEL_WIDTH + MODEL_WIDTH * width),
            transcendentals=0,
        ),
        name=f"norm_project_{part}",
    )(z, own, *below, *above, *far, gain, *weights, cos, sin)


def attend_kernel(tile, info_ref, first_ref, qa_ref, qb_ref, w_hbm, *refs):
    sources, refs = refs[: 18 * PARTS], refs[18 * PARTS :]
    outs, refs = refs[: 9 * PARTS], refs[9 * PARTS :]
    k_buf, v_buf, w_ref, top_ref, total_ref, mix_ref, sem, w_sem = refs
    wide, z = info_ref[16], info_ref[17]
    columns = qa_ref.shape[1]
    rows = tile // SIDE_X
    heads = columns // rows
    factor = math.log2(math.e) / math.sqrt(HEAD_SIZE)
    line = SIDE_Y * CORES
    x, y, c = wide // line, wide % line // CORES, wide % CORES

    copies = []
    for p in range(PARTS):
        for i, buf in enumerate((k_buf, v_buf)):
            held = sources[18 * p + 9 * i : 18 * p + 9 * i + 9]
            half = held[7].shape[0]
            for n, (ref, step, row) in enumerate(
                [(ref, step & 7, 0) for ref, step in zip(held, (0, 1, 2, 3, -1, -2, -3, 4))] + [(held[8], 4, half)]
            ):
                to = buf.at[p, step, pl.ds(row, ref.shape[0]), :]
                copies.append(pltpu.make_async_copy(ref, to, sem.at[p, i, n]))
    w_copy = pltpu.make_async_copy(w_hbm, w_ref, w_sem)
    for copy in copies:
        copy.start()
    w_copy.start()
    for copy in copies:
        copy.wait()

    def gray(d):
        return d ^ (d >> 1)

    def load(j):
        block, yc = j // line, j % line
        keys, values = [], []
        for from_x in range(SIDE_X):
            away = (from_x - block) & 3
            p, a = away & 1, away >> 1
            row = (gray((x - from_x) & 3) * GROUPS + a) * rows
            keys.append(k_buf[p, (wide - yc) & 7, pl.ds(pl.multiple_of(row, rows), rows), :])
            row = (gray((y - yc // CORES) & 3) * GROUPS + a) * HEAD_SIZE
            step = (x * CORES + c - from_x * CORES - yc % CORES) & 7
            values.append(v_buf[p, step, pl.ds(pl.multiple_of(row, HEAD_SIZE), HEAD_SIZE), :])
        return jnp.concatenate(keys, axis=0), jnp.concatenate(values, axis=1)

    mixed = []
    for g in range(PARTS * GROUPS):
        q_ref = (qa_ref, qb_ref)[g // GROUPS]
        low, own, base, late = (info_ref[4 * i + g] for i in range(4))
        top_ref[...] = jnp.full(top_ref.shape, NEGATIVE, jnp.float32)
        total_ref[...] = jnp.zeros(total_ref.shape, jnp.float32)
        mix_ref[...] = jnp.zeros(mix_ref.shape, jnp.float32)

        def step(j, masked):
            keys, values = load(j)
            for left in range(0, columns, SPAN):
                span = slice(left, left + SPAN)
                scores = lax.dot_general(keys, q_ref[g % GROUPS, span, :], _NT, preferred_element_type=jnp.float32)
                if masked:
                    key_pos = j * tile + lax.broadcasted_iota(jnp.int32, (tile, SPAN), 0)
                    query_pos = base + (lax.broadcasted_iota(jnp.int32, (1, SPAN), 1) & (rows - 1))
                    allowed = (key_pos >= first_ref[g, :, span]) & (key_pos <= query_pos)
                    scores = jnp.where(allowed, scores, NEGATIVE)
                old = top_ref[:, span]
                new = jnp.maximum(old, jnp.max(scores, axis=0, keepdims=True))
                weights = jnp.exp2(scores * factor - new * factor)
                shrink = jnp.exp2((old - new) * factor)
                top_ref[:, span] = new
                total_ref[:, span] = total_ref[:, span] * shrink + jnp.sum(weights, axis=0, keepdims=True)
                mix_ref[:, span] = mix_ref[:, span] * shrink + jnp.dot(
                    values, weights.astype(jnp.bfloat16), preferred_element_type=jnp.float32
                )

        step(own, True)
        clear = jnp.minimum((late + tile - 1) // tile, own)
        lax.fori_loop(low, clear, lambda j, _: (step(j, True), 0)[1], 0)
        lax.fori_loop(clear, own, lambda j, _: (step(j, False), 0)[1], 0)
        total = mix_ref[...] / total_ref[...]
        mixed.append(
            jnp.concatenate([total[:, h * rows : (h + 1) * rows].T.astype(jnp.bfloat16) for h in range(heads)], axis=1)
        )
    mixed = jnp.concatenate(mixed, axis=0)
    w_copy.wait()

    narrow = 8
    width = w_ref.shape[1] // narrow
    part_rows = mixed.shape[0] // PARTS
    for at, ahead in ((7, 4), (3, 3), (6, -3), (2, 2), (5, -2), (1, 1), (4, -1), (0, 0)):
        target = (z + ahead) & (narrow - 1)
        block = jnp.dot(
            mixed, w_ref[:, pl.ds(pl.multiple_of(target * width, width), width)], preferred_element_type=jnp.float32
        ).astype(jnp.bfloat16)
        for p in range(PARTS):
            part = block[p * part_rows : (p + 1) * part_rows]
            if at < 7:
                outs[9 * p + at][...] = part
            else:
                outs[9 * p + 7][...] = part[: part_rows // 2]
                outs[9 * p + 8][...] = part[part_rows // 2 :]


def attend(info, first, queries, w_out, sources, tile, tiles):
    columns = queries[0].shape[1]
    rows = tile // PARTS
    width = w_out.shape[1] // 8
    block = lambda n: jax.ShapeDtypeStruct((n, width), jnp.bfloat16)
    return pl.pallas_call(
        functools.partial(attend_kernel, tile),
        in_specs=[SMEM] + [VMEM] * 3 + [ANYWHERE] * (1 + len(sources)),
        out_specs=[VMEM] * 9 * PARTS,
        out_shape=([block(rows)] * 7 + [block(rows // 2)] * 2) * PARTS,
        scratch_shapes=[
            pltpu.VMEM((PARTS, 8, *sources[0].shape), jnp.bfloat16),
            pltpu.VMEM((PARTS, 8, *sources[9].shape), jnp.bfloat16),
            pltpu.VMEM(w_out.shape, jnp.bfloat16),
            pltpu.VMEM((1, columns), jnp.float32),
            pltpu.VMEM((1, columns), jnp.float32),
            pltpu.VMEM((HEAD_SIZE, columns), jnp.float32),
            pltpu.SemaphoreType.DMA((PARTS, 2, 9)),
            pltpu.SemaphoreType.DMA,
        ],
        compiler_params=pltpu.CompilerParams(vmem_limit_bytes=ATTEND_VMEM),
        cost_estimate=pl.CostEstimate(
            flops=4 * columns * HEAD_SIZE * tiles * tile,
            bytes_accessed=2 * (2 * tiles * tile * HEAD_SIZE + w_out.size),
            transcendentals=columns * tiles * tile,
        ),
        name="attend",
    )(info, first, *queries, w_out, *sources)


def add_rounded(a, *others):
    total = a.astype(jnp.float32)
    for b in others:
        total = total + b.astype(jnp.float32)
    return total.astype(jnp.bfloat16)


def ring_scatter(blocks, up, down):
    own, u1, u2, u3, d1, d2, d3, far_u, far_d = blocks
    half = far_u.shape[0]
    got = lax.ppermute(far_u, "narrow", up), lax.ppermute(far_d, "narrow", down)
    rising = jnp.concatenate([add_rounded(u3[:half], got[0]), u3[half:]])
    falling = jnp.concatenate([d3[:half], add_rounded(d3[half:], got[1])])
    for u, d in ((u2, d2), (u1, d1), (None, None)):
        rising, falling = lax.ppermute(rising, "narrow", up), lax.ppermute(falling, "narrow", down)
        if u is not None:
            rising, falling = add_rounded(u, rising), add_rounded(d, falling)
    return add_rounded(own, rising, falling)


def per_device(wide, narrow, tokens, norm_gain, w_query, key_weight, value_weight, w_out, doc_lengths):
    rows = tokens.shape[0]
    wide_index = lax.axis_index("wide")
    z = lax.axis_index("narrow")
    heads = w_query.shape[1] // HEAD_SIZE
    z_up = [(i, (i + 1) % narrow) for i in range(narrow)]
    z_down = [(b, a) for a, b in z_up]

    gain = norm_gain.reshape(1, -1)
    for bit in (1, 2, 4):
        other = lax.ppermute(gain, "narrow", [(i, i ^ bit) for i in range(narrow)])
        gain = jnp.where(
            (z & bit) != 0, jnp.concatenate([other, gain], axis=1), jnp.concatenate([gain, other], axis=1)
        )
    weights = (w_query, key_weight, value_weight)

    x_pairs, y_pairs, yc_pairs, xc_pairs = (
        ring_pairs(wide, shift) for shift in (shift_x, shift_y, shift_yc, shift_xc)
    )
    line = SIDE_Y * CORES
    x = wide_index // line
    group_rows = rows // SIDE_X

    def along_x(away):
        return [(i, shift_x(i, away)) for i in range(wide)]

    with jax.named_scope("deal_tokens"):
        groups = []
        for away in AWAY:
            piece = lax.dynamic_slice_in_dim(tokens, (x + away) % SIDE_X * group_rows, group_rows, 0)
            groups.append(lax.ppermute(piece, "wide", along_x(away)) if away else piece)

    with jax.named_scope("positions"):
        docs = doc_lengths.shape[0]
        earlier = jnp.arange(docs)[None, :] < jnp.arange(docs)[:, None]
        starts = jnp.sum(jnp.where(earlier, doc_lengths[None, :], 0), axis=1)
        blocks = (x - jnp.array(AWAY, jnp.int32)) % SIDE_X * line + wide_index % line
        bases = blocks * rows + x * group_rows
        positions = (bases[:, None] + jnp.arange(group_rows, dtype=jnp.int32)[None, :]).reshape(-1)
        first = jnp.max(
            jnp.where(starts[None, :] <= positions[:, None], starts[None, :], 0), axis=1
        ).astype(jnp.int32)
        half = HEAD_SIZE // 2
        frequency = ROPE_BASE ** (-(jnp.arange(half, dtype=jnp.float32) * 2.0 / HEAD_SIZE))
        angles = (positions - first).astype(jnp.float32)[:, None] * frequency[None, :]
        cosine, sine = jnp.cos(angles), jnp.sin(angles)
        cos = jnp.concatenate([cosine, cosine], axis=1)
        sin = jnp.concatenate([-sine, sine], axis=1)
        first = first.reshape(len(AWAY), 1, group_rows)
        info = jnp.concatenate(
            [
                first[:, 0, 0] // rows,
                blocks,
                bases,
                first[:, 0, -1],
                wide_index.reshape(1),
                z.reshape(1),
            ]
        ).astype(jnp.int32)
        first = jnp.tile(first, (1, 1, heads))

    queries, sources = [], []
    held = None
    for part in range(PARTS):
        own = jnp.concatenate(groups[part * GROUPS : (part + 1) * GROUPS], axis=0)
        if held is not None:
            own, _ = lax.optimization_barrier((own, held))
        with jax.named_scope(f"gather_tokens_{part}"):
            gathered = ring_gather(own, "narrow", z_up, z_down, narrow)
        held = (gathered[0][-1], gathered[1][-1])
        q, k, vt = project(part, z.reshape(1), own, gathered, gain, weights, cos, sin, heads)
        queries.append(q)
        with jax.named_scope(f"gather_keys_values_{part}"):
            b, a, far = ring_gather(k, "wide", *x_pairs, SIDE_X)
            keys = jnp.concatenate([k, *b, *a, *far], axis=0)
            b, a, far = ring_gather(vt, "wide", *y_pairs, SIDE_Y)
            values = jnp.concatenate([vt, *b, *a, *far], axis=0)
            b, a, far = ring_gather(keys, "wide", *yc_pairs, SIDE_Y * CORES)
            sources += [keys, *b, *a, *far]
            b, a, far = ring_gather(values, "wide", *xc_pairs, SIDE_X * CORES)
            sources += [values, *b, *a, *far]

    sums = attend(info, first, queries, w_out, sources, rows, wide)
    back = []
    for part in range(PARTS):
        with jax.named_scope(f"sum_heads_{part}"):
            total = ring_scatter(sums[9 * part : 9 * part + 9], z_up, z_down)
        with jax.named_scope(f"deal_back_{part}"):
            for a in range(GROUPS):
                away = AWAY[part * GROUPS + a]
                piece = total[a * group_rows : (a + 1) * group_rows]
                back.append(lax.ppermute(piece, "wide", along_x(-away)) if away else piece)
    with jax.named_scope("lay_out"):
        order = [back[AWAY.index(k)] for k in (0, 1, 2, -1)]
        return lax.dynamic_slice_in_dim(jnp.concatenate(order + order[:-1], axis=0), (-x) % SIDE_X * group_rows, rows, 0)


def solution(mesh):
    in_specs = (
        P("wide", "narrow"),
        P("narrow"),
        P(None, "narrow"),
        P(None, "narrow"),
        P(None, "narrow"),
        P("narrow", None),
        P(),
    )
    return jax.shard_map(
        functools.partial(per_device, mesh.shape["wide"], mesh.shape["narrow"]),
        mesh=mesh,
        in_specs=in_specs,
        out_specs=P("wide", "narrow"),
        check_vma=False,
    )
```

```python
import functools
import math

import jax
import jax.numpy as jnp
from jax import lax
from jax.experimental import pallas as pl
from jax.experimental.pallas import tpu as pltpu
from jax.sharding import PartitionSpec as P

MODEL_WIDTH = 4096
HEAD_SIZE = 128
EPSILON = 1e-05
ROPE_BASE = 500000.0
NEGATIVE = -1e30
MIB = 1024 * 1024
SIDE_X, SIDE_Y, CORES, SIDE_Z = 4, 4, 2, 8
LINE = SIDE_Y * CORES
QUARTERS = SIDE_X
AWAY = (0, 1, 2, -1)
STEPS = (0, 1, 2, 3, -1, -2, -3, 4)

_NT = (((1,), (1,)), ((), ()))
VMEM = pl.BlockSpec(memory_space=pltpu.VMEM)
SMEM = pl.BlockSpec(memory_space=pltpu.SMEM)
ANYWHERE = pl.BlockSpec(memory_space=pl.ANY)


def shift_x(i, by):
    return (i // LINE + by) % SIDE_X * LINE + i % LINE


def shift_y(i, by):
    y = (i // CORES % SIDE_Y + by) % SIDE_Y
    return i // LINE * LINE + y * CORES + i % CORES


def ring_gather(x, axis, up, down, count):
    below, above = [], []
    for _ in range(count // 2 - 1):
        below.append(lax.ppermute(below[-1] if below else x, axis, up))
        above.append(lax.ppermute(above[-1] if above else x, axis, down))
    half = x.shape[0] // 2
    far = [lax.ppermute(below[-1][:half], axis, up), lax.ppermute(above[-1][half:], axis, down)]
    return below, above, far


def project_kernel(
    place_ref, own, b1, b2, b3, a1, a2, a3, far_b, far_a, gain_ref, wq_hbm, wk_hbm, wv_hbm, cos_ref, sin_ref,
    q_ref, keep_ref, send_ref, normed_ref, wq_ref, wk_ref, wv_ref, sem,
):
    copies = [
        pltpu.make_async_copy(hbm, ref, sem.at[i])
        for i, (hbm, ref) in enumerate(((wk_hbm, wk_ref), (wv_hbm, wv_ref), (wq_hbm, wq_ref)))
    ]
    for copy in copies:
        copy.start()
    z, core = place_ref[0], place_ref[1]
    rows, width = own.shape
    quarter = rows // QUARTERS
    heads = q_ref.shape[1] // quarter
    near = list(zip(STEPS, (own, b1, b2, b3, a1, a2, a3)))
    for s in range(QUARTERS):
        here = slice(s * quarter, (s + 1) * quarter)
        far = (far_b, far_a)[s // 2]
        views = [(k, ref, here) for k, ref in near] + [(4, far, slice(s % 2 * quarter, (s % 2 + 1) * quarter))]
        squares = jnp.zeros((quarter, 1), jnp.float32)
        for _, ref, span in views:
            x = ref[span, :].astype(jnp.float32)
            squares = squares + jnp.sum(x * x, axis=1, keepdims=True)
        inverse = lax.rsqrt(squares / MODEL_WIDTH + EPSILON)
        for k, ref, span in views:
            columns = pl.ds(pl.multiple_of(((z - k) & (SIDE_Z - 1)) * width, width), width)
            x = ref[span, :].astype(jnp.float32)
            normed_ref[here, columns] = (x * inverse * gain_ref[:, columns]).astype(jnp.bfloat16)

    def turned(head, here):
        return (head * cos_ref[here, :] + pltpu.roll(head, HEAD_SIZE // 2, 1) * sin_ref[here, :]).astype(jnp.bfloat16)

    for copy in copies:
        copy.wait()
    normed = normed_ref[...]
    raw_k = jnp.dot(normed, wk_ref[...], preferred_element_type=jnp.float32)
    raw_v = jnp.dot(normed, wv_ref[...], preferred_element_type=jnp.float32)
    for s in range(QUARTERS):
        here = slice(s * quarter, (s + 1) * quarter)
        keys = turned(raw_k[here], here)
        values = raw_v[here].T.astype(jnp.bfloat16)
        keep_ref[here, :] = jnp.where(core == 0, keys, values)
        send_ref[here, :] = jnp.where(core == 0, values, keys)
    for h in range(0, heads, 2):
        pair = jnp.dot(normed, wq_ref[:, h * HEAD_SIZE : (h + 2) * HEAD_SIZE], preferred_element_type=jnp.float32)
        for n in range(2):
            for s in range(QUARTERS):
                here = slice(s * quarter, (s + 1) * quarter)
                head = pair[here, n * HEAD_SIZE : (n + 1) * HEAD_SIZE]
                q_ref[s, (h + n) * quarter : (h + n + 1) * quarter, :] = turned(head, here)


def project(place, own, gathered, gain, weights, cos, sin, heads):
    below, above, far = gathered
    rows, width = own.shape[0], sum(w.shape[1] for w in weights)
    quarter = rows // QUARTERS
    block = jax.ShapeDtypeStruct((rows, HEAD_SIZE), jnp.bfloat16)
    return pl.pallas_call(
        project_kernel,
        in_specs=[SMEM] + [VMEM] * 10 + [ANYWHERE] * 3 + [VMEM] * 2,
        out_specs=[VMEM] * 3,
        out_shape=[jax.ShapeDtypeStruct((QUARTERS, heads * quarter, HEAD_SIZE), jnp.bfloat16), block, block],
        scratch_shapes=[pltpu.VMEM((rows, MODEL_WIDTH), jnp.bfloat16)]
        + [pltpu.VMEM(w.shape, jnp.bfloat16) for w in weights]
        + [pltpu.SemaphoreType.DMA((3,))],
        compiler_params=pltpu.CompilerParams(vmem_limit_bytes=48 * MIB),
        cost_estimate=pl.CostEstimate(
            flops=2 * rows * MODEL_WIDTH * width,
            bytes_accessed=2 * (rows * MODEL_WIDTH + MODEL_WIDTH * width),
            transcendentals=0,
        ),
        name="norm_project",
    )(place, own, *below, *above, *far, gain, *weights, cos, sin)


def gray(d):
    return d ^ (d >> 1)


def attend_groups(groups, info_ref, first_ref, q_refs, out_refs, k_buf, v_buf, top_ref, total_ref, mix_ref):
    wide = info_ref[16]
    columns = q_refs[0].shape[0]
    tile = k_buf.shape[1] // (SIDE_X * CORES)
    rows = tile // QUARTERS
    heads = columns // rows
    factor = math.log2(math.e) / math.sqrt(HEAD_SIZE)
    x, y = wide // LINE, wide % LINE // CORES

    def load(j):
        dx, dy, core = (x - j // LINE) & 3, (y - j % LINE // CORES) & 3, j % CORES
        row = pl.multiple_of((gray(dx) * CORES + core) * tile, tile)
        keys = k_buf[gray(dy), pl.ds(row, tile), :]
        row = pl.multiple_of((gray(dy) * CORES + core) * tile, tile)
        values = [v_buf[gray(dx), pl.ds(row + s * HEAD_SIZE, HEAD_SIZE), :] for s in range(QUARTERS)]
        return keys, jnp.concatenate(values, axis=1)

    for g, q_ref, out_ref in zip(groups, q_refs, out_refs):
        low, own, base, late = (info_ref[4 * i + g] for i in range(4))
        top_ref[...] = jnp.full(top_ref.shape, NEGATIVE, jnp.float32)
        total_ref[...] = jnp.zeros(total_ref.shape, jnp.float32)
        mix_ref[...] = jnp.zeros(mix_ref.shape, jnp.float32)

        def step(j, tiles, masked):
            held = [load(j + n) for n in range(tiles)]
            keys = jnp.concatenate([k for k, _ in held], axis=0)
            values = jnp.concatenate([v for _, v in held], axis=1)
            scores = lax.dot_general(keys, q_ref[...], _NT, preferred_element_type=jnp.float32)
            if masked:
                key_pos = j * tile + lax.broadcasted_iota(jnp.int32, (tile * tiles, columns), 0)
                query_pos = base + (lax.broadcasted_iota(jnp.int32, (1, columns), 1) & (rows - 1))
                allowed = (key_pos >= first_ref[g]) & (key_pos <= query_pos)
                scores = jnp.where(allowed, scores, NEGATIVE)
            old = top_ref[...]
            new = jnp.maximum(old, jnp.max(scores, axis=0, keepdims=True))
            weights = jnp.exp2(scores * factor - new * factor)
            shrink = jnp.exp2((old - new) * factor)
            top_ref[...] = new
            total_ref[...] = total_ref[...] * shrink + jnp.sum(weights, axis=0, keepdims=True)
            mix_ref[...] = mix_ref[...] * shrink + jnp.dot(
                values, weights.astype(jnp.bfloat16), preferred_element_type=jnp.float32
            )

        step(own, 1, True)
        clear = jnp.minimum((late + tile - 1) // tile, own)
        pairs = (own - clear) // 2
        lax.fori_loop(low, clear, lambda j, _: (step(j, 1, True), 0)[1], 0)
        lax.fori_loop(0, pairs, lambda n, _: (step(clear + 2 * n, 2, False), 0)[1], 0)

        @pl.when(clear + 2 * pairs < own)
        def _():
            step(own - 1, 1, False)

        mixed = mix_ref[...] / total_ref[...]
        for h in range(heads):
            out_ref[:, h * HEAD_SIZE : (h + 1) * HEAD_SIZE] = mixed[:, h * rows : (h + 1) * rows].T.astype(jnp.bfloat16)


def attend_kernel(groups, info_ref, first_ref, *refs):
    count = len(groups)
    q_refs, mine, other, refs = refs[:count], refs[count : count + 5], refs[count + 5 : count + 10], refs[count + 10 :]
    out_refs, (k_buf, v_buf, top_ref, total_ref, mix_ref, sem) = refs[:count], refs[count:]
    core = info_ref[16] & 1
    spans = [(0, 0), (1, 0), (2, 0), (3, 0), (3, mine[3].shape[0])]

    def copies(keys, values):
        return [
            pltpu.make_async_copy(ref, buf.at[step, pl.ds(row, ref.shape[0]), :], sem.at[i, n])
            for i, (refs, buf) in enumerate(((keys, k_buf), (values, v_buf)))
            for n, (ref, (step, row)) in enumerate(zip(refs, spans))
        ]

    @pl.when(core == 0)
    def _():
        for copy in copies(mine, other):
            copy.start()

    @pl.when(core != 0)
    def _():
        for copy in copies(other, mine):
            copy.start()

    for copy in copies(mine, other):
        copy.wait()
    attend_groups(groups, info_ref, first_ref, q_refs, out_refs, k_buf, v_buf, top_ref, total_ref, mix_ref)


def attend(groups, info, first, queries, held, heads, name):
    columns = queries[0].shape[0]
    tile = columns * QUARTERS // heads
    keys = SIDE_X * SIDE_Y * CORES * tile
    count = len(groups)
    return pl.pallas_call(
        functools.partial(attend_kernel, groups),
        in_specs=[SMEM] + [VMEM] * (1 + count) + [ANYWHERE] * len(held),
        out_specs=[VMEM] * count,
        out_shape=[jax.ShapeDtypeStruct((tile // QUARTERS, heads * HEAD_SIZE), jnp.bfloat16)] * count,
        scratch_shapes=[
            pltpu.VMEM((4, *held[0].shape), jnp.bfloat16),
            pltpu.VMEM((4, *held[0].shape), jnp.bfloat16),
            pltpu.VMEM((1, columns), jnp.float32),
            pltpu.VMEM((1, columns), jnp.float32),
            pltpu.VMEM((HEAD_SIZE, columns), jnp.float32),
            pltpu.SemaphoreType.DMA((2, 5)),
        ],
        compiler_params=pltpu.CompilerParams(vmem_limit_bytes=50 * MIB),
        cost_estimate=pl.CostEstimate(
            flops=4 * count * columns * HEAD_SIZE * keys // 2,
            bytes_accessed=2 * 2 * keys * HEAD_SIZE,
            transcendentals=count * columns * keys // 2,
        ),
        name=name,
    )(info, first, *queries, *held)


TRAVELLING = [(ahead, part) for ahead in (4, 3, -3, 2, -2, 1, -1) for part in range(2)]


def product_kernel(place_ref, m0, m1, m2, m3, w_ref, *refs):
    outs, own_ref, mixed_ref = dict(zip(TRAVELLING, refs)), refs[-2], refs[-1]
    z, x = place_ref[0], place_ref[2]
    quarter = m0.shape[0]
    for away, ref in zip(AWAY, (m0, m1, m2, m3)):
        row = ((x + away) & (QUARTERS - 1)) * quarter
        mixed_ref[pl.ds(pl.multiple_of(row, quarter), quarter), :] = ref[...]
    mixed = mixed_ref[...]
    width = w_ref.shape[1] // SIDE_Z
    half = mixed.shape[0] // 2
    for ahead in (4, 3, -3, 2, -2, 1, -1, 0):
        columns = pl.ds(pl.multiple_of(((z + ahead) & (SIDE_Z - 1)) * width, width), width)
        block = jnp.dot(mixed, w_ref[:, columns], preferred_element_type=jnp.float32).astype(jnp.bfloat16)
        if ahead == 0:
            own_ref[...] = block
        else:
            outs[ahead, 0][...] = block[:half]
            outs[ahead, 1][...] = block[half:]


def product(place, pieces, w_out):
    rows, features = pieces[0].shape[0] * QUARTERS, pieces[0].shape[1]
    width = w_out.shape[1] // SIDE_Z
    block = lambda n: jax.ShapeDtypeStruct((n, width), jnp.bfloat16)
    return pl.pallas_call(
        product_kernel,
        in_specs=[SMEM] + [VMEM] * 5,
        out_specs=[VMEM] * 15,
        out_shape=[block(rows // 2)] * 14 + [block(rows)],
        scratch_shapes=[pltpu.VMEM((rows, features), jnp.bfloat16)],
        compiler_params=pltpu.CompilerParams(vmem_limit_bytes=16 * MIB),
        cost_estimate=pl.CostEstimate(
            flops=2 * rows * features * w_out.shape[1],
            bytes_accessed=2 * (rows * features + w_out.size + rows * w_out.shape[1]),
            transcendentals=0,
        ),
        name="output_product",
    )(place, *pieces, w_out)


def add_rounded(a, *others):
    total = a.astype(jnp.float32)
    for b in others:
        total = total + b.astype(jnp.float32)
    return total.astype(jnp.bfloat16)


def ring_scatter(blocks, own, up, down):
    streams = {
        (1, 0): [4, 3, 2, 1],
        (-1, 1): [4, -3, -2, -1],
        (1, 1): [3, 2, 1],
        (-1, 0): [-3, -2, -1],
    }
    carried = {}
    for hop in range(4):
        for key, stops in streams.items():
            if hop < len(stops):
                block = blocks[stops[hop], key[1]]
                if key in carried:
                    block = add_rounded(block, carried[key])
                carried[key] = lax.ppermute(block, "narrow", up if key[0] > 0 else down)
    half = own.shape[0] // 2
    return jnp.concatenate(
        [add_rounded(own[part * half : (part + 1) * half], carried[1, part], carried[-1, part]) for part in range(2)]
    )


def per_device(wide, narrow, tokens, norm_gain, w_query, key_weight, value_weight, w_out, doc_lengths):
    rows = tokens.shape[0]
    wide_index = lax.axis_index("wide")
    z = lax.axis_index("narrow")
    x, core = wide_index // LINE, wide_index % CORES
    heads = w_query.shape[1] // HEAD_SIZE
    quarter = rows // QUARTERS
    z_up = [(i, (i + 1) % narrow) for i in range(narrow)]
    z_down = [(b, a) for a, b in z_up]
    place = jnp.stack([z, core, x]).astype(jnp.int32)

    with jax.named_scope("gather_tokens"):
        gathered = ring_gather(tokens, "narrow", z_up, z_down, narrow)
    with jax.named_scope("gather_gain"):
        gain = norm_gain.reshape(1, -1)
        for bit in (1, 2, 4):
            other = lax.ppermute(gain, "narrow", [(i, i ^ bit) for i in range(narrow)])
            gain = jnp.where(
                (z & bit) != 0, jnp.concatenate([other, gain], axis=1), jnp.concatenate([gain, other], axis=1)
            )

    with jax.named_scope("positions"):
        docs = doc_lengths.shape[0]
        earlier = jnp.arange(docs)[None, :] < jnp.arange(docs)[:, None]
        starts = jnp.sum(jnp.where(earlier, doc_lengths[None, :], 0), axis=1)

        def first_of(positions):
            return jnp.max(
                jnp.where(starts[None, :] <= positions[:, None], starts[None, :], 0), axis=1
            ).astype(jnp.int32)

        positions = wide_index * rows + jnp.arange(rows, dtype=jnp.int32)
        half = HEAD_SIZE // 2
        frequency = ROPE_BASE ** (-(jnp.arange(half, dtype=jnp.float32) * 2.0 / HEAD_SIZE))
        angles = (positions - first_of(positions)).astype(jnp.float32)[:, None] * frequency[None, :]
        cosine, sine = jnp.cos(angles), jnp.sin(angles)
        cos = jnp.concatenate([cosine, cosine], axis=1)
        sin = jnp.concatenate([-sine, sine], axis=1)

        blocks = (x - jnp.array(AWAY, jnp.int32)) % SIDE_X * LINE + wide_index % LINE
        bases = blocks * rows + x * quarter
        first = first_of((bases[:, None] + jnp.arange(quarter, dtype=jnp.int32)[None, :]).reshape(-1))
        first = first.reshape(len(AWAY), 1, quarter)
        info = jnp.concatenate(
            [first[:, 0, 0] // rows, blocks, bases, first[:, 0, -1], wide_index.reshape(1)]
        ).astype(jnp.int32)
        first = jnp.tile(first, (1, 1, heads))

    q, keep, send = project(
        place, tokens, gathered, gain, (w_query, key_weight, value_weight), cos, sin, heads
    )

    def by_core(of_keys, of_values):
        up = [(i, (of_values if i % CORES else of_keys)(i, 1)) for i in range(wide)]
        return up, [(b, a) for a, b in up]

    swap = [(i, i ^ 1) for i in range(wide)]
    with jax.named_scope("gather_keys_values"):
        received = lax.ppermute(send, "wide", swap)
        base = jnp.where(
            core == 0, jnp.concatenate([keep, received], axis=0), jnp.concatenate([received, keep], axis=0)
        )
        below, above, far = ring_gather(base, "wide", *by_core(shift_x, shift_y), SIDE_X)
        base = jnp.concatenate([base, *below, *above, *far], axis=0)
        below, above, far = ring_gather(base, "wide", *by_core(shift_y, shift_x), SIDE_X)
        mine = [base, *below, *above, *far]
        other = [lax.ppermute(block, "wide", swap) for block in mine]

    def along_x(away):
        return [(i, shift_x(i, away)) for i in range(wide)]

    with jax.named_scope("deal_queries"):
        queries = []
        for away in AWAY:
            piece = lax.dynamic_index_in_dim(q, (x + away) % SIDE_X, 0, keepdims=False)
            queries.append(lax.ppermute(piece, "wide", along_x(away)) if away else piece)

    mixed = attend((1, 2, 3), info, first, queries[1:], mine + other, heads, "attend_far")
    with jax.named_scope("deal_heads"):
        mixed = [lax.ppermute(piece, "wide", along_x(-away)) for away, piece in zip(AWAY[1:], mixed)]
    (own,) = attend((0,), info, first, queries[:1], mine + other, heads, "attend_own")

    *sums, total = product(place, [own, *mixed], w_out)
    with jax.named_scope("sum_heads"):
        return ring_scatter(dict(zip(TRAVELLING, sums)), total, z_up, z_down)


def solution(mesh):
    in_specs = (
        P("wide", "narrow"),
        P("narrow"),
        P(None, "narrow"),
        P(None, "narrow"),
        P(None, "narrow"),
        P("narrow", None),
        P(),
    )
    return jax.shard_map(
        functools.partial(per_device, mesh.shape["wide"], mesh.shape["narrow"]),
        mesh=mesh,
        in_specs=in_specs,
        out_specs=P("wide", "narrow"),
        check_vma=False,
    )
```

```python
import functools
import math

import jax
import jax.numpy as jnp
from jax import lax
from jax.experimental import pallas as pl
from jax.experimental.pallas import tpu as pltpu
from jax.sharding import PartitionSpec as P

MODEL_WIDTH = 4096
HEAD_SIZE = 128
EPSILON = 1e-05
ROPE_BASE = 500000.0
NEGATIVE = -1e30
MIB = 1024 * 1024
SIDE_X, SIDE_Y, CORES, SIDE_Z = 4, 4, 2, 8
LINE = SIDE_Y * CORES
QUARTERS = SIDE_X
AWAY = (0, 1, 2, -1)
HEADER = 16
STEPS = (0, 1, 2, 3, -1, -2, -3, 4)

_NT = (((1,), (1,)), ((), ()))
VMEM = pl.BlockSpec(memory_space=pltpu.VMEM)
SMEM = pl.BlockSpec(memory_space=pltpu.SMEM)
ANYWHERE = pl.BlockSpec(memory_space=pl.ANY)


def shift_x(i, by):
    return (i // LINE + by) % SIDE_X * LINE + i % LINE


def shift_y(i, by):
    y = (i // CORES % SIDE_Y + by) % SIDE_Y
    return i // LINE * LINE + y * CORES + i % CORES


def ring_gather(x, axis, up, down, count, cut):
    below, above = [], []
    for _ in range(count // 2 - 1):
        below.append(lax.ppermute(below[-1] if below else x, axis, up))
        above.append(lax.ppermute(above[-1] if above else x, axis, down))
    far = [lax.ppermute(below[-1][:cut], axis, up), lax.ppermute(above[-1][cut:], axis, down)]
    return below, above, far


def turned(head, cos, sin):
    return (head * cos + pltpu.roll(head, HEAD_SIZE // 2, 1) * sin).astype(jnp.bfloat16)


def norm_kernel(
    place_ref, own, b1, b2, b3, a1, a2, a3, far_b, far_a, wk_hbm, wv_hbm, cos_ref, sin_ref,
    keep_ref, send_ref, normed_hbm, x_ref, normed_ref, wk_ref, wv_ref, x_sem, sem, out_sem,
):
    z, core = place_ref[0], place_ref[1]
    rows, width = normed_ref.shape[0], own.shape[1]
    quarter = rows // QUARTERS
    near = (own, b1, b2, b3, a1, a2, a3)
    cut = far_b.shape[0]

    def fetch(s):
        start, size = (0, HEADER + quarter) if s == 0 else (HEADER + s * quarter, quarter)
        far, at = (far_b, start) if start < cut else (far_a, start - cut)
        parts = [(ref, start) for ref in near] + [(far, at)]
        return [
            pltpu.make_async_copy(
                ref.at[pl.ds(row, size), :], x_ref.at[n, pl.ds(start, size), :], x_sem.at[s, n]
            )
            for n, (ref, row) in enumerate(parts)
        ]

    for s in range(QUARTERS):
        for copy in fetch(s):
            copy.start()
    copies = [
        pltpu.make_async_copy(hbm, ref, sem.at[i]) for i, (hbm, ref) in enumerate(((wk_hbm, wk_ref), (wv_hbm, wv_ref)))
    ]
    for copy in copies:
        copy.start()

    gains, stores = [], []
    for s in range(QUARTERS):
        for copy in fetch(s):
            copy.wait()
        if s == 0:
            for n in range(SIDE_Z):
                parts = x_ref[n, :HEADER, :].astype(jnp.float32)
                gains.append(parts[0:1] + (parts[1:2] + parts[2:3]))
        here = slice(s * quarter, (s + 1) * quarter)
        moved = slice(HEADER + s * quarter, HEADER + (s + 1) * quarter)
        squares = jnp.zeros((quarter, 1), jnp.float32)
        for n in range(SIDE_Z):
            x = x_ref[n, moved, :].astype(jnp.float32)
            squares = squares + jnp.sum(x * x, axis=1, keepdims=True)
        inverse = lax.rsqrt(squares / MODEL_WIDTH + EPSILON)
        for n, k in enumerate(STEPS):
            columns = pl.ds(pl.multiple_of(((z - k) & (SIDE_Z - 1)) * width, width), width)
            x = x_ref[n, moved, :].astype(jnp.float32)
            normed_ref[here, columns] = (x * inverse * gains[n]).astype(jnp.bfloat16)
        stores.append(pltpu.make_async_copy(normed_ref.at[here, :], normed_hbm.at[here, :], out_sem.at[s]))
        stores[-1].start()

    for copy in copies:
        copy.wait()
    normed = normed_ref[...]
    raw_k = jnp.dot(normed, wk_ref[...], preferred_element_type=jnp.float32)
    raw_v = jnp.dot(normed, wv_ref[...], preferred_element_type=jnp.float32)
    for s in range(QUARTERS):
        here = slice(s * quarter, (s + 1) * quarter)
        keys = turned(raw_k[here], cos_ref[here, :], sin_ref[here, :])
        values = raw_v[here].T.astype(jnp.bfloat16)
        keep_ref[here, :] = jnp.where(core == 0, keys, values)
        send_ref[here, :] = jnp.where(core == 0, values, keys)
    for copy in stores:
        copy.wait()


def norm_project(place, own, gathered, weights, cos, sin):
    below, above, far = gathered
    rows, width = cos.shape[0], sum(w.shape[1] for w in weights)
    block = jax.ShapeDtypeStruct((rows, HEAD_SIZE), jnp.bfloat16)
    return pl.pallas_call(
        norm_kernel,
        in_specs=[SMEM] + [ANYWHERE] * 11 + [VMEM] * 2,
        out_specs=[VMEM, VMEM, ANYWHERE],
        out_shape=[block, block, jax.ShapeDtypeStruct((rows, MODEL_WIDTH), jnp.bfloat16)],
        scratch_shapes=[
            pltpu.VMEM((SIDE_Z, *own.shape), jnp.bfloat16),
            pltpu.VMEM((rows, MODEL_WIDTH), jnp.bfloat16),
            *(pltpu.VMEM(w.shape, jnp.bfloat16) for w in weights),
            pltpu.SemaphoreType.DMA((QUARTERS, SIDE_Z)),
            pltpu.SemaphoreType.DMA((2,)),
            pltpu.SemaphoreType.DMA((QUARTERS,)),
        ],
        compiler_params=pltpu.CompilerParams(vmem_limit_bytes=54 * MIB),
        cost_estimate=pl.CostEstimate(
            flops=2 * rows * MODEL_WIDTH * width,
            bytes_accessed=2 * (2 * rows * MODEL_WIDTH + MODEL_WIDTH * width),
            transcendentals=0,
        ),
        name="norm_project",
    )(place, own, *below, *above, *far, *weights, cos, sin)


def query_kernel(normed_hbm, w_hbm, cos_ref, sin_ref, q_ref, normed_ref, w_ref, sem):
    quarter = normed_ref.shape[0] // QUARTERS
    heads = w_ref.shape[1] // HEAD_SIZE
    copies = [pltpu.make_async_copy(normed_hbm, normed_ref, sem.at[0])]
    for h in range(0, heads, 2):
        pair = pl.ds(h * HEAD_SIZE, 2 * HEAD_SIZE)
        copies.append(pltpu.make_async_copy(w_hbm.at[:, pair], w_ref.at[:, pair], sem.at[1 + h // 2]))
    for copy in copies:
        copy.start()
    copies[0].wait()
    normed = normed_ref[...]
    for h in range(0, heads, 2):
        copies[1 + h // 2].wait()
        pair = jnp.dot(normed, w_ref[:, h * HEAD_SIZE : (h + 2) * HEAD_SIZE], preferred_element_type=jnp.float32)
        for n in range(2):
            for s in range(QUARTERS):
                here = slice(s * quarter, (s + 1) * quarter)
                head = pair[here, n * HEAD_SIZE : (n + 1) * HEAD_SIZE]
                q_ref[s, (h + n) * quarter : (h + n + 1) * quarter, :] = turned(head, cos_ref[here, :], sin_ref[here, :])


def query_project(normed, weight, cos, sin):
    rows, width = normed.shape[0], weight.shape[1]
    shape = (QUARTERS, width // HEAD_SIZE * (rows // QUARTERS), HEAD_SIZE)
    return pl.pallas_call(
        query_kernel,
        in_specs=[ANYWHERE] * 2 + [VMEM] * 2,
        out_specs=VMEM,
        out_shape=jax.ShapeDtypeStruct(shape, jnp.bfloat16),
        scratch_shapes=[
            pltpu.VMEM(normed.shape, jnp.bfloat16),
            pltpu.VMEM(weight.shape, jnp.bfloat16),
            pltpu.SemaphoreType.DMA((1 + width // (2 * HEAD_SIZE),)),
        ],
        compiler_params=pltpu.CompilerParams(vmem_limit_bytes=54 * MIB),
        cost_estimate=pl.CostEstimate(
            flops=2 * rows * MODEL_WIDTH * width,
            bytes_accessed=2 * (rows * MODEL_WIDTH + MODEL_WIDTH * width),
            transcendentals=0,
        ),
        name="query_project",
    )(normed, weight, cos, sin)


def gray(d):
    return d ^ (d >> 1)


def attend_groups(groups, info_ref, first_ref, q_refs, out_refs, k_buf, v_buf, top_ref, total_ref, mix_ref):
    wide = info_ref[16]
    columns = q_refs[0].shape[0]
    tile = k_buf.shape[1] // (SIDE_X * CORES)
    rows = tile // QUARTERS
    heads = columns // rows
    factor = math.log2(math.e) / math.sqrt(HEAD_SIZE)
    x, y = wide // LINE, wide % LINE // CORES

    def load(j):
        dx, dy, core = (x - j // LINE) & 3, (y - j % LINE // CORES) & 3, j % CORES
        row = pl.multiple_of((gray(dx) * CORES + core) * tile, tile)
        keys = k_buf[gray(dy), pl.ds(row, tile), :]
        row = pl.multiple_of((gray(dy) * CORES + core) * tile, tile)
        values = [v_buf[gray(dx), pl.ds(row + s * HEAD_SIZE, HEAD_SIZE), :] for s in range(QUARTERS)]
        return keys, jnp.concatenate(values, axis=1)

    for g, q_ref, out_ref in zip(groups, q_refs, out_refs):
        low, own, base, late = (info_ref[4 * i + g] for i in range(4))
        top_ref[...] = jnp.full(top_ref.shape, NEGATIVE, jnp.float32)
        total_ref[...] = jnp.zeros(total_ref.shape, jnp.float32)
        mix_ref[...] = jnp.zeros(mix_ref.shape, jnp.float32)

        def step(j, tiles, masked):
            held = [load(j + n) for n in range(tiles)]
            keys = jnp.concatenate([k for k, _ in held], axis=0)
            values = jnp.concatenate([v for _, v in held], axis=1)
            scores = lax.dot_general(keys, q_ref[...], _NT, preferred_element_type=jnp.float32)
            if masked:
                key_pos = j * tile + lax.broadcasted_iota(jnp.int32, (tile * tiles, columns), 0)
                query_pos = base + (lax.broadcasted_iota(jnp.int32, (1, columns), 1) & (rows - 1))
                allowed = (key_pos >= first_ref[g]) & (key_pos <= query_pos)
                scores = jnp.where(allowed, scores, NEGATIVE)
            old = top_ref[...]
            new = jnp.maximum(old, jnp.max(scores, axis=0, keepdims=True))
            weights = jnp.exp2(scores * factor - new * factor)
            shrink = jnp.exp2((old - new) * factor)
            top_ref[...] = new
            total_ref[...] = total_ref[...] * shrink + jnp.sum(weights, axis=0, keepdims=True)
            mix_ref[...] = mix_ref[...] * shrink + jnp.dot(
                values, weights.astype(jnp.bfloat16), preferred_element_type=jnp.float32
            )

        step(own, 1, True)
        clear = jnp.minimum((late + tile - 1) // tile, own)
        pairs = (own - clear) // 2
        lax.fori_loop(low, clear, lambda j, _: (step(j, 1, True), 0)[1], 0)
        lax.fori_loop(0, pairs, lambda n, _: (step(clear + 2 * n, 2, False), 0)[1], 0)

        @pl.when(clear + 2 * pairs < own)
        def _():
            step(own - 1, 1, False)

        mixed = mix_ref[...] / total_ref[...]
        for h in range(heads):
            out_ref[:, h * HEAD_SIZE : (h + 1) * HEAD_SIZE] = mixed[:, h * rows : (h + 1) * rows].T.astype(jnp.bfloat16)


def attend_kernel(groups, info_ref, first_ref, *refs):
    count = len(groups)
    q_refs, mine, other, refs = refs[:count], refs[count : count + 8], refs[count + 8 : count + 16], refs[count + 16 :]
    out_refs, (k_buf, v_buf, top_ref, total_ref, mix_ref, sem) = refs[:count], refs[count:]
    core = info_ref[16] & 1
    spans = [(n // 2, n % 2 * mine[0].shape[0]) for n in range(8)]

    def copies(keys, values):
        return [
            pltpu.make_async_copy(ref, buf.at[step, pl.ds(row, ref.shape[0]), :], sem.at[i, n])
            for i, (refs, buf) in enumerate(((keys, k_buf), (values, v_buf)))
            for n, (ref, (step, row)) in enumerate(zip(refs, spans))
        ]

    @pl.when(core == 0)
    def _():
        for copy in copies(mine, other):
            copy.start()

    @pl.when(core != 0)
    def _():
        for copy in copies(other, mine):
            copy.start()

    for copy in copies(mine, other):
        copy.wait()
    attend_groups(groups, info_ref, first_ref, q_refs, out_refs, k_buf, v_buf, top_ref, total_ref, mix_ref)


def attend(groups, info, first, queries, held, heads, name):
    columns = queries[0].shape[0]
    tile = columns * QUARTERS // heads
    keys = SIDE_X * SIDE_Y * CORES * tile
    count = len(groups)
    return pl.pallas_call(
        functools.partial(attend_kernel, groups),
        in_specs=[SMEM] + [VMEM] * (1 + count) + [ANYWHERE] * len(held),
        out_specs=[VMEM] * count,
        out_shape=[jax.ShapeDtypeStruct((tile // QUARTERS, heads * HEAD_SIZE), jnp.bfloat16)] * count,
        scratch_shapes=[
            pltpu.VMEM((4, 2 * held[0].shape[0], HEAD_SIZE), jnp.bfloat16),
            pltpu.VMEM((4, 2 * held[0].shape[0], HEAD_SIZE), jnp.bfloat16),
            pltpu.VMEM((1, columns), jnp.float32),
            pltpu.VMEM((1, columns), jnp.float32),
            pltpu.VMEM((HEAD_SIZE, columns), jnp.float32),
            pltpu.SemaphoreType.DMA((2, 8)),
        ],
        compiler_params=pltpu.CompilerParams(vmem_limit_bytes=50 * MIB),
        cost_estimate=pl.CostEstimate(
            flops=4 * count * columns * HEAD_SIZE * keys // 2,
            bytes_accessed=2 * 2 * keys * HEAD_SIZE,
            transcendentals=count * columns * keys // 2,
        ),
        name=name,
    )(info, first, *queries, *held)


def product_kernel(aheads, place_ref, m0, m1, m2, m3, w_ref, *refs):
    outs, mixed_ref = iter(refs), refs[-1]
    z, x = place_ref[0], place_ref[2]
    quarter = m0.shape[0]
    for away, ref in zip(AWAY, (m0, m1, m2, m3)):
        row = ((x + away) & (QUARTERS - 1)) * quarter
        mixed_ref[pl.ds(pl.multiple_of(row, quarter), quarter), :] = ref[...]
    mixed = mixed_ref[...]
    width = w_ref.shape[1] // SIDE_Z
    half = mixed.shape[0] // 2
    for ahead in aheads:
        columns = pl.ds(pl.multiple_of(((z + ahead) & (SIDE_Z - 1)) * width, width), width)
        block = jnp.dot(mixed, w_ref[:, columns], preferred_element_type=jnp.float32).astype(jnp.bfloat16)
        next(outs)[...] = block[:half]
        next(outs)[...] = block[half:]


def product(aheads, place, pieces, w_out, name):
    rows, features = pieces[0].shape[0] * QUARTERS, pieces[0].shape[1]
    width = w_out.shape[1] // SIDE_Z
    block = lambda n: jax.ShapeDtypeStruct((n, width), jnp.bfloat16)
    sums = pl.pallas_call(
        functools.partial(product_kernel, aheads),
        in_specs=[SMEM] + [VMEM] * 5,
        out_specs=[VMEM] * 2 * len(aheads),
        out_shape=[block(rows // 2)] * 2 * len(aheads),
        scratch_shapes=[pltpu.VMEM((rows, features), jnp.bfloat16)],
        compiler_params=pltpu.CompilerParams(vmem_limit_bytes=16 * MIB),
        cost_estimate=pl.CostEstimate(
            flops=2 * rows * features * width * len(aheads),
            bytes_accessed=2 * (rows * features + (features + rows) * width * len(aheads)),
            transcendentals=0,
        ),
        name=name,
    )(place, *pieces, w_out)
    return {(ahead, part): sums[2 * n + part] for n, ahead in enumerate(aheads) for part in range(2)}


def add_rounded(a, *others):
    total = a.astype(jnp.float32)
    for b in others:
        total = total + b.astype(jnp.float32)
    return total.astype(jnp.bfloat16)


def ring_scatter(blocks, up, down):
    streams = {
        (1, 0): [4, 3, 2, 1],
        (-1, 1): [4, -3, -2, -1],
        (1, 1): [3, 2, 1],
        (-1, 0): [-3, -2, -1],
    }
    carried = {}
    for hop in range(4):
        for key, stops in streams.items():
            if hop < len(stops):
                block = blocks[stops[hop], key[1]]
                if key in carried:
                    block = add_rounded(block, carried[key])
                carried[key] = lax.ppermute(block, "narrow", up if key[0] > 0 else down)
    return jnp.concatenate([add_rounded(blocks[0, part], carried[1, part], carried[-1, part]) for part in range(2)])


def per_device(wide, narrow, tokens, norm_gain, w_query, key_weight, value_weight, w_out, doc_lengths):
    rows = tokens.shape[0]
    wide_index = lax.axis_index("wide")
    z = lax.axis_index("narrow")
    x, core = wide_index // LINE, wide_index % CORES
    heads = w_query.shape[1] // HEAD_SIZE
    quarter = rows // QUARTERS
    z_up = [(i, (i + 1) % narrow) for i in range(narrow)]
    z_down = [(b, a) for a, b in z_up]
    place = jnp.stack([z, core, x]).astype(jnp.int32)

    with jax.named_scope("gather_tokens"):
        gain = norm_gain.reshape(1, -1)
        parts = []
        for _ in range(3):
            parts.append(lax.reduce_precision(gain, 8, 7))
            gain = gain - parts[-1]
        header = jnp.concatenate(parts + [jnp.zeros((HEADER - 3, gain.shape[1]), jnp.float32)], axis=0)
        block = jnp.concatenate([header.astype(jnp.bfloat16), tokens], axis=0)
        gathered = ring_gather(block, "narrow", z_up, z_down, narrow, HEADER + rows // 2)

    with jax.named_scope("positions"):
        docs = doc_lengths.shape[0]
        earlier = jnp.arange(docs)[None, :] < jnp.arange(docs)[:, None]
        starts = jnp.sum(jnp.where(earlier, doc_lengths[None, :], 0), axis=1)

        def first_of(positions):
            return jnp.max(
                jnp.where(starts[None, :] <= positions[:, None], starts[None, :], 0), axis=1
            ).astype(jnp.int32)

        positions = wide_index * rows + jnp.arange(rows, dtype=jnp.int32)
        half = HEAD_SIZE // 2
        frequency = ROPE_BASE ** (-(jnp.arange(half, dtype=jnp.float32) * 2.0 / HEAD_SIZE))
        angles = (positions - first_of(positions)).astype(jnp.float32)[:, None] * frequency[None, :]
        cosine, sine = jnp.cos(angles), jnp.sin(angles)
        cos = jnp.concatenate([cosine, cosine], axis=1)
        sin = jnp.concatenate([-sine, sine], axis=1)

        blocks = (x - jnp.array(AWAY, jnp.int32)) % SIDE_X * LINE + wide_index % LINE
        bases = blocks * rows + x * quarter
        first = first_of((bases[:, None] + jnp.arange(quarter, dtype=jnp.int32)[None, :]).reshape(-1))
        first = first.reshape(len(AWAY), 1, quarter)
        info = jnp.concatenate(
            [first[:, 0, 0] // rows, blocks, bases, first[:, 0, -1], wide_index.reshape(1)]
        ).astype(jnp.int32)
        first = jnp.tile(first, (1, 1, heads))

    cos, sin, first, info, place = lax.optimization_barrier((cos, sin, first, info, place))
    keep, send, normed = norm_project(place, block, gathered, (key_weight, value_weight), cos, sin)
    def by_core(of_keys, of_values):
        up = [(i, (of_values if i % CORES else of_keys)(i, 1)) for i in range(wide)]
        return up, [(b, a) for a, b in up]

    swap = [(i, i ^ 1) for i in range(wide)]
    with jax.named_scope("gather_keys_values"):
        received = lax.ppermute(send, "wide", swap)
        base = jnp.where(
            core == 0, jnp.concatenate([keep, received], axis=0), jnp.concatenate([received, keep], axis=0)
        )
        below, above, far = ring_gather(base, "wide", *by_core(shift_x, shift_y), SIDE_X, rows)
        low, high = jnp.concatenate([base, *below], axis=0), jnp.concatenate([*above, *far], axis=0)
        up, down = by_core(shift_y, shift_x)
        move = lambda block, pairs: lax.ppermute(block, "wide", pairs)
        mine = [low, high, move(low, up), move(high, up), move(low, down), move(high, down)]
        q = query_project(normed, w_query, cos, sin)
        mine += [move(mine[2], up), move(mine[5], down)]
        other = [move(block, swap) for block in mine]
        q, _ = lax.optimization_barrier((q, mine[2:6]))

    def along_x(away):
        return [(i, shift_x(i, away)) for i in range(wide)]

    with jax.named_scope("deal_queries"):
        queries = []
        for away in AWAY:
            piece = lax.dynamic_index_in_dim(q, (x + away) % SIDE_X, 0, keepdims=False)
            queries.append(lax.ppermute(piece, "wide", along_x(away)) if away else piece)

    mixed = attend((1, 2, 3), info, first, queries[1:], mine + other, heads, "attend_far")
    with jax.named_scope("deal_heads"):
        mixed = [lax.ppermute(piece, "wide", along_x(-away)) for away, piece in zip(AWAY[1:], mixed)]
    (own,) = attend((0,), info, first, queries[:1], mine + other, heads, "attend_own")

    sums = product((4, 3, -3), place, [own, *mixed], w_out, "output_product_first")
    sums |= product((2, -2, 1, -1, 0), place, [own, *mixed], w_out, "output_product_rest")
    with jax.named_scope("sum_heads"):
        return ring_scatter(sums, z_up, z_down)


def solution(mesh):
    in_specs = (
        P("wide", "narrow"),
        P("narrow"),
        P(None, "narrow"),
        P(None, "narrow"),
        P(None, "narrow"),
        P("narrow", None),
        P(),
    )
    return jax.shard_map(
        functools.partial(per_device, mesh.shape["wide"], mesh.shape["narrow"]),
        mesh=mesh,
        in_specs=in_specs,
        out_specs=P("wide", "narrow"),
        check_vma=False,
    )
```

```python
import functools
import math

import jax
import jax.numpy as jnp
from jax import lax
from jax.experimental import pallas as pl
from jax.experimental.pallas import tpu as pltpu
from jax.sharding import PartitionSpec as P

MODEL_WIDTH = 4096
HEAD_SIZE = 128
EPSILON = 1e-05
ROPE_BASE = 500000.0
NEGATIVE = -1e30
MIB = 1024 * 1024
SIDE_X, SIDE_Y, CORES, SIDE_Z = 4, 4, 2, 8
LINE = SIDE_Y * CORES
QUARTERS = SIDE_X
AWAY = (0, 1, 2, -1)
STEPS = (0, 1, 2, 3, -1, -2, -3, 4)

_NT = (((1,), (1,)), ((), ()))
VMEM = pl.BlockSpec(memory_space=pltpu.VMEM)
SMEM = pl.BlockSpec(memory_space=pltpu.SMEM)
ANYWHERE = pl.BlockSpec(memory_space=pl.ANY)


def shift_x(i, by):
    return (i // LINE + by) % SIDE_X * LINE + i % LINE


def shift_y(i, by):
    y = (i // CORES % SIDE_Y + by) % SIDE_Y
    return i // LINE * LINE + y * CORES + i % CORES


def ring_gather(x, axis, up, down, count):
    below, above = [], []
    for _ in range(count // 2 - 1):
        below.append(lax.ppermute(below[-1] if below else x, axis, up))
        above.append(lax.ppermute(above[-1] if above else x, axis, down))
    half = x.shape[0] // 2
    far = [lax.ppermute(below[-1][:half], axis, up), lax.ppermute(above[-1][half:], axis, down)]
    return below, above, far


def ring_streams(low, high, axis, up, down, count):
    streams = {
        (True, False): [low],
        (False, True): [high],
        (True, True): [high],
        (False, False): [low],
    }
    for hop in range(count // 2):
        for (is_up, is_high), held in streams.items():
            if hop < count // 2 - 1 or is_up != is_high:
                held.append(lax.ppermute(held[-1], axis, up if is_up else down))
    blocks = [(low, high)]
    for is_up in (True, False):
        blocks += [(streams[is_up, False][n], streams[is_up, True][n]) for n in range(1, count // 2)]
    blocks.append((streams[True, False][count // 2], streams[False, True][count // 2]))
    return blocks


def project_kernel(
    place_ref, gain_ref, cos_ref, sin_ref, wq_hbm, wk_hbm, wv_hbm, *refs
):
    x_refs, (q_ref, keep_ref, send_ref, normed_ref, wq_ref, wk_ref, wv_ref, sem) = refs[: 2 * SIDE_Z], refs[2 * SIDE_Z :]
    copies = [
        pltpu.make_async_copy(hbm, ref, sem.at[i])
        for i, (hbm, ref) in enumerate(((wk_hbm, wk_ref), (wv_hbm, wv_ref), (wq_hbm, wq_ref)))
    ]
    for copy in copies:
        copy.start()
    z, core = place_ref[0], place_ref[1]
    rows, width = normed_ref.shape[0], x_refs[0].shape[1]
    quarter = rows // QUARTERS
    heads = q_ref.shape[1] // quarter
    for s in range(QUARTERS):
        here = slice(s * quarter, (s + 1) * quarter)
        span = slice(s % 2 * quarter, (s % 2 + 1) * quarter)
        views = [(k, x_refs[2 * n + s // 2], span) for n, k in enumerate(STEPS)]
        squares = jnp.zeros((quarter, HEAD_SIZE), jnp.float32)
        for _, ref, span in views:
            x = ref[span, :].astype(jnp.float32)
            for lane in range(0, width, HEAD_SIZE):
                piece = x[:, lane : lane + HEAD_SIZE]
                squares = squares + piece * piece
        inverse = lax.rsqrt(jnp.sum(squares, axis=1, keepdims=True) / MODEL_WIDTH + EPSILON)
        for k, ref, span in views:
            columns = pl.ds(pl.multiple_of(((z - k) & (SIDE_Z - 1)) * width, width), width)
            x = ref[span, :].astype(jnp.float32)
            normed_ref[here, columns] = (x * inverse * gain_ref[:, columns]).astype(jnp.bfloat16)

    def turned(head, here):
        return (head * cos_ref[here, :] + pltpu.roll(head, HEAD_SIZE // 2, 1) * sin_ref[here, :]).astype(jnp.bfloat16)

    for copy in copies:
        copy.wait()
    normed = normed_ref[...]
    raw_k = jnp.dot(normed, wk_ref[...], preferred_element_type=jnp.float32)
    raw_v = jnp.dot(normed, wv_ref[...], preferred_element_type=jnp.float32)
    for s in range(QUARTERS):
        here = slice(s * quarter, (s + 1) * quarter)
        keys = turned(raw_k[here], here)
        values = raw_v[here].T.astype(jnp.bfloat16)
        keep_ref[here, :] = jnp.where(core == 0, keys, values)
        send_ref[here, :] = jnp.where(core == 0, values, keys)
    for h in range(0, heads, 2):
        pair = jnp.dot(normed, wq_ref[:, h * HEAD_SIZE : (h + 2) * HEAD_SIZE], preferred_element_type=jnp.float32)
        for n in range(2):
            for s in range(QUARTERS):
                here = slice(s * quarter, (s + 1) * quarter)
                head = pair[here, n * HEAD_SIZE : (n + 1) * HEAD_SIZE]
                q_ref[s, (h + n) * quarter : (h + n + 1) * quarter, :] = turned(head, here)


def project(place, gathered, gain, weights, cos, sin, heads):
    gathered = [half for block in gathered for half in block]
    rows, width = cos.shape[0], sum(w.shape[1] for w in weights)
    quarter = rows // QUARTERS
    block = jax.ShapeDtypeStruct((rows, HEAD_SIZE), jnp.bfloat16)
    return pl.pallas_call(
        project_kernel,
        in_specs=[SMEM] + [VMEM] * 3 + [ANYWHERE] * 3 + [VMEM] * len(gathered),
        out_specs=[VMEM] * 3,
        out_shape=[jax.ShapeDtypeStruct((QUARTERS, heads * quarter, HEAD_SIZE), jnp.bfloat16), block, block],
        scratch_shapes=[pltpu.VMEM((rows, MODEL_WIDTH), jnp.bfloat16)]
        + [pltpu.VMEM(w.shape, jnp.bfloat16) for w in weights]
        + [pltpu.SemaphoreType.DMA((3,))],
        compiler_params=pltpu.CompilerParams(vmem_limit_bytes=56 * MIB),
        cost_estimate=pl.CostEstimate(
            flops=2 * rows * MODEL_WIDTH * width,
            bytes_accessed=2 * (rows * MODEL_WIDTH + MODEL_WIDTH * width),
            transcendentals=0,
        ),
        name="norm_project",
    )(place, gain, cos, sin, *weights, *gathered)


def gray(d):
    return d ^ (d >> 1)


def attend_groups(groups, wait_rest, info_ref, first_ref, q_refs, out_refs, k_buf, v_buf, top_ref, total_ref, mix_ref):
    wide = info_ref[16]
    columns = q_refs[0].shape[0]
    tile = k_buf.shape[1] // (SIDE_X * CORES)
    rows = tile // QUARTERS
    heads = columns // rows
    factor = math.log2(math.e) / math.sqrt(HEAD_SIZE)
    x, y = wide // LINE, wide % LINE // CORES

    def load(j):
        dx, dy, core = (x - j // LINE) & 3, (y - j % LINE // CORES) & 3, j % CORES
        row = pl.multiple_of((gray(dx) * CORES + core) * tile, tile)
        keys = k_buf[gray(dy), pl.ds(row, tile), :]
        row = pl.multiple_of((gray(dy) * CORES + core) * tile, tile)
        values = [v_buf[gray(dx), pl.ds(row + s * HEAD_SIZE, HEAD_SIZE), :] for s in range(QUARTERS)]
        return keys, jnp.concatenate(values, axis=1)

    for g, q_ref, out_ref in zip(groups, q_refs, out_refs):
        low, own, base, late = (info_ref[4 * i + g] for i in range(4))
        top_ref[...] = jnp.full(top_ref.shape, NEGATIVE, jnp.float32)
        total_ref[...] = jnp.zeros(total_ref.shape, jnp.float32)
        mix_ref[...] = jnp.zeros(mix_ref.shape, jnp.float32)

        def step(j, tiles, masked):
            held = [load(j + n) for n in range(tiles)]
            keys = jnp.concatenate([k for k, _ in held], axis=0)
            values = jnp.concatenate([v for _, v in held], axis=1)
            scores = lax.dot_general(keys, q_ref[...], _NT, preferred_element_type=jnp.float32)
            if masked:
                key_pos = j * tile + lax.broadcasted_iota(jnp.int32, (tile * tiles, columns), 0)
                query_pos = base + (lax.broadcasted_iota(jnp.int32, (1, columns), 1) & (rows - 1))
                allowed = (key_pos >= first_ref[g]) & (key_pos <= query_pos)
                scores = jnp.where(allowed, scores, NEGATIVE)
            old = top_ref[...]
            new = jnp.maximum(old, jnp.max(scores, axis=0, keepdims=True))
            weights = jnp.exp2(scores * factor - new * factor)
            shrink = jnp.exp2((old - new) * factor)
            top_ref[...] = new
            total_ref[...] = total_ref[...] * shrink + jnp.sum(weights, axis=0, keepdims=True)
            mix_ref[...] = mix_ref[...] * shrink + jnp.dot(
                values, weights.astype(jnp.bfloat16), preferred_element_type=jnp.float32
            )

        step(own, 1, True)
        if g == groups[0]:
            wait_rest()
        clear = jnp.minimum((late + tile - 1) // tile, own)
        pairs = (own - clear) // 2
        lax.fori_loop(low, clear, lambda j, _: (step(j, 1, True), 0)[1], 0)
        lax.fori_loop(0, pairs, lambda n, _: (step(clear + 2 * n, 2, False), 0)[1], 0)

        @pl.when(clear + 2 * pairs < own)
        def _():
            step(own - 1, 1, False)

        mixed = mix_ref[...] / total_ref[...]
        for h in range(heads):
            out_ref[:, h * HEAD_SIZE : (h + 1) * HEAD_SIZE] = mixed[:, h * rows : (h + 1) * rows].T.astype(jnp.bfloat16)


def attend_kernel(groups, info_ref, first_ref, *refs):
    count = len(groups)
    q_refs, mine, other, refs = refs[:count], refs[count : count + 5], refs[count + 5 : count + 10], refs[count + 10 :]
    out_refs, (k_buf, v_buf, top_ref, total_ref, mix_ref, sem) = refs[:count], refs[count:]
    core = info_ref[16] & 1
    spans = [(0, 0), (1, 0), (2, 0), (3, 0), (3, mine[3].shape[0])]

    def copies(keys, values):
        return [
            pltpu.make_async_copy(ref, buf.at[step, pl.ds(row, ref.shape[0]), :], sem.at[i, n])
            for i, (refs, buf) in enumerate(((keys, k_buf), (values, v_buf)))
            for n, (ref, (step, row)) in enumerate(zip(refs, spans))
        ]

    @pl.when(core == 0)
    def _():
        started = copies(mine, other)
        for copy in (started[0], *started[5:], *started[1:5]):
            copy.start()

    @pl.when(core != 0)
    def _():
        started = copies(other, mine)
        for copy in (started[0], *started[5:], *started[1:5]):
            copy.start()

    waits = copies(mine, other)
    for copy in (waits[0], *waits[5:]):
        copy.wait()

    def wait_rest():
        for copy in waits[1:5]:
            copy.wait()

    attend_groups(groups, wait_rest, info_ref, first_ref, q_refs, out_refs, k_buf, v_buf, top_ref, total_ref, mix_ref)


def attend(groups, info, first, queries, held, heads, name):
    columns = queries[0].shape[0]
    tile = columns * QUARTERS // heads
    keys = SIDE_X * SIDE_Y * CORES * tile
    count = len(groups)
    return pl.pallas_call(
        functools.partial(attend_kernel, groups),
        in_specs=[SMEM] + [VMEM] * (1 + count) + [ANYWHERE] * len(held),
        out_specs=[VMEM] * count,
        out_shape=[jax.ShapeDtypeStruct((tile // QUARTERS, heads * HEAD_SIZE), jnp.bfloat16)] * count,
        scratch_shapes=[
            pltpu.VMEM((4, *held[0].shape), jnp.bfloat16),
            pltpu.VMEM((4, *held[0].shape), jnp.bfloat16),
            pltpu.VMEM((1, columns), jnp.float32),
            pltpu.VMEM((1, columns), jnp.float32),
            pltpu.VMEM((HEAD_SIZE, columns), jnp.float32),
            pltpu.SemaphoreType.DMA((2, 5)),
        ],
        compiler_params=pltpu.CompilerParams(vmem_limit_bytes=50 * MIB),
        cost_estimate=pl.CostEstimate(
            flops=4 * count * columns * HEAD_SIZE * keys // 2,
            bytes_accessed=2 * 2 * keys * HEAD_SIZE,
            transcendentals=count * columns * keys // 2,
        ),
        name=name,
    )(info, first, *queries, *held)


def product_kernel(aheads, place_ref, m0, m1, m2, m3, w_ref, *refs):
    outs, mixed_ref = iter(refs), refs[-1]
    z, x = place_ref[0], place_ref[2]
    quarter = m0.shape[0]
    for away, ref in zip(AWAY, (m0, m1, m2, m3)):
        row = ((x + away) & (QUARTERS - 1)) * quarter
        mixed_ref[pl.ds(pl.multiple_of(row, quarter), quarter), :] = ref[...]
    mixed = mixed_ref[...]
    width = w_ref.shape[1] // SIDE_Z
    half = mixed.shape[0] // 2
    for ahead in aheads:
        columns = pl.ds(pl.multiple_of(((z + ahead) & (SIDE_Z - 1)) * width, width), width)
        block = jnp.dot(mixed, w_ref[:, columns], preferred_element_type=jnp.float32).astype(jnp.bfloat16)
        next(outs)[...] = block[:half]
        next(outs)[...] = block[half:]


def product(aheads, place, pieces, w_out, name):
    rows, features = pieces[0].shape[0] * QUARTERS, pieces[0].shape[1]
    width = w_out.shape[1] // SIDE_Z
    block = lambda n: jax.ShapeDtypeStruct((n, width), jnp.bfloat16)
    sums = pl.pallas_call(
        functools.partial(product_kernel, aheads),
        in_specs=[SMEM] + [VMEM] * 5,
        out_specs=[VMEM] * 2 * len(aheads),
        out_shape=[block(rows // 2)] * 2 * len(aheads),
        scratch_shapes=[pltpu.VMEM((rows, features), jnp.bfloat16)],
        compiler_params=pltpu.CompilerParams(vmem_limit_bytes=16 * MIB),
        cost_estimate=pl.CostEstimate(
            flops=2 * rows * features * width * len(aheads),
            bytes_accessed=2 * (rows * features + (features + rows) * width * len(aheads)),
            transcendentals=0,
        ),
        name=name,
    )(place, *pieces, w_out)
    return {(ahead, part): sums[2 * n + part] for n, ahead in enumerate(aheads) for part in range(2)}


def add_rounded(a, *others):
    total = a.astype(jnp.float32)
    for b in others:
        total = total + b.astype(jnp.float32)
    return total.astype(jnp.bfloat16)


def ring_scatter(blocks, up, down):
    streams = {
        (1, 0): [4, 3, 2, 1],
        (-1, 1): [4, -3, -2, -1],
        (1, 1): [3, 2, 1],
        (-1, 0): [-3, -2, -1],
    }
    carried = {}
    for hop in range(4):
        for key, stops in streams.items():
            if hop < len(stops):
                block = blocks[stops[hop], key[1]]
                if key in carried:
                    block = add_rounded(block, carried[key])
                carried[key] = lax.ppermute(block, "narrow", up if key[0] > 0 else down)
    return jnp.concatenate([add_rounded(blocks[0, part], carried[1, part], carried[-1, part]) for part in range(2)])


def per_device(wide, narrow, tokens, norm_gain, w_query, key_weight, value_weight, w_out, doc_lengths):
    rows = tokens.shape[0]
    wide_index = lax.axis_index("wide")
    z = lax.axis_index("narrow")
    x, core = wide_index // LINE, wide_index % CORES
    heads = w_query.shape[1] // HEAD_SIZE
    quarter = rows // QUARTERS
    z_up = [(i, (i + 1) % narrow) for i in range(narrow)]
    z_down = [(b, a) for a, b in z_up]
    place = jnp.stack([z, core, x]).astype(jnp.int32)

    with jax.named_scope("gather_tokens"):
        gathered = ring_streams(tokens[: rows // 2], tokens[rows // 2 :], "narrow", z_up, z_down, narrow)
    with jax.named_scope("gather_gain"):
        gain = norm_gain.reshape(1, -1)
        for bit in (1, 2, 4):
            other = lax.ppermute(gain, "narrow", [(i, i ^ bit) for i in range(narrow)])
            gain = jnp.where(
                (z & bit) != 0, jnp.concatenate([other, gain], axis=1), jnp.concatenate([gain, other], axis=1)
            )

    with jax.named_scope("positions"):
        docs = doc_lengths.shape[0]
        earlier = jnp.arange(docs)[None, :] < jnp.arange(docs)[:, None]
        starts = jnp.sum(jnp.where(earlier, doc_lengths[None, :], 0), axis=1)

        def first_of(positions):
            return jnp.max(
                jnp.where(starts[None, :] <= positions[:, None], starts[None, :], 0), axis=1
            ).astype(jnp.int32)

        positions = wide_index * rows + jnp.arange(rows, dtype=jnp.int32)
        half = HEAD_SIZE // 2
        frequency = ROPE_BASE ** (-(jnp.arange(half, dtype=jnp.float32) * 2.0 / HEAD_SIZE))
        angles = (positions - first_of(positions)).astype(jnp.float32)[:, None] * frequency[None, :]
        cosine, sine = jnp.cos(angles), jnp.sin(angles)
        cos = jnp.concatenate([cosine, cosine], axis=1)
        sin = jnp.concatenate([-sine, sine], axis=1)

        blocks = (x - jnp.array(AWAY, jnp.int32)) % SIDE_X * LINE + wide_index % LINE
        bases = blocks * rows + x * quarter
        first = first_of((bases[:, None] + jnp.arange(quarter, dtype=jnp.int32)[None, :]).reshape(-1))
        first = first.reshape(len(AWAY), 1, quarter)
        info = jnp.concatenate(
            [first[:, 0, 0] // rows, blocks, bases, first[:, 0, -1], wide_index.reshape(1)]
        ).astype(jnp.int32)
        first = jnp.tile(first, (1, 1, heads))

    cos, sin, first, info, place = lax.optimization_barrier((cos, sin, first, info, place))
    q, keep, send = project(
        place, gathered, gain, (w_query, key_weight, value_weight), cos, sin, heads
    )

    def by_core(of_keys, of_values):
        up = [(i, (of_values if i % CORES else of_keys)(i, 1)) for i in range(wide)]
        return up, [(b, a) for a, b in up]

    swap = [(i, i ^ 1) for i in range(wide)]
    with jax.named_scope("gather_keys_values"):
        received = lax.ppermute(send, "wide", swap)
        base = jnp.where(
            core == 0, jnp.concatenate([keep, received], axis=0), jnp.concatenate([received, keep], axis=0)
        )
        below, above, far = ring_gather(base, "wide", *by_core(shift_x, shift_y), SIDE_X)
        base = jnp.concatenate([base, *below, *above, *far], axis=0)
        below, above, far = ring_gather(base, "wide", *by_core(shift_y, shift_x), SIDE_X)
        mine = [base, *below, *above, *far]
        other = [lax.ppermute(block, "wide", swap) for block in mine]

    def along_x(away):
        return [(i, shift_x(i, away)) for i in range(wide)]

    with jax.named_scope("deal_queries"):
        queries = []
        for away in AWAY:
            piece = lax.dynamic_index_in_dim(q, (x + away) % SIDE_X, 0, keepdims=False)
            queries.append(lax.ppermute(piece, "wide", along_x(away)) if away else piece)

    mixed = attend((1, 2, 3), info, first, queries[1:], mine + other, heads, "attend_far")
    with jax.named_scope("deal_heads"):
        mixed = [lax.ppermute(piece, "wide", along_x(-away)) for away, piece in zip(AWAY[1:], mixed)]
    (own,) = attend((0,), info, first, queries[:1], mine + other, heads, "attend_own")

    sums = product((4, 3, -3), place, [own, *mixed], w_out, "output_product_first")
    sums |= product((2, -2, 1, -1, 0), place, [own, *mixed], w_out, "output_product_rest")
    with jax.named_scope("sum_heads"):
        return ring_scatter(sums, z_up, z_down)


def solution(mesh):
    in_specs = (
        P("wide", "narrow"),
        P("narrow"),
        P(None, "narrow"),
        P(None, "narrow"),
        P(None, "narrow"),
        P("narrow", None),
        P(),
    )
    return jax.shard_map(
        functools.partial(per_device, mesh.shape["wide"], mesh.shape["narrow"]),
        mesh=mesh,
        in_specs=in_specs,
        out_specs=P("wide", "narrow"),
        check_vma=False,
    )
```

```python
import functools
import math

import jax
import jax.numpy as jnp
from jax import lax
from jax.experimental import pallas as pl
from jax.experimental.pallas import tpu as pltpu
from jax.sharding import PartitionSpec as P

MODEL_WIDTH = 4096
HEAD_SIZE = 128
EPSILON = 1e-05
ROPE_BASE = 500000.0
NEGATIVE = -1e30
MIB = 1024 * 1024
SIDE_X, SIDE_Y, CORES, SIDE_Z = 4, 4, 2, 8
LINE = SIDE_Y * CORES
QUARTERS = SIDE_X
AWAY = (0, 1, 2, -1)
STEPS = (0, 1, 2, 3, -1, -2, -3, 4)

_NT = (((1,), (1,)), ((), ()))
VMEM = pl.BlockSpec(memory_space=pltpu.VMEM)
SMEM = pl.BlockSpec(memory_space=pltpu.SMEM)
ANYWHERE = pl.BlockSpec(memory_space=pl.ANY)


def shift_x(i, by):
    return (i // LINE + by) % SIDE_X * LINE + i % LINE


def shift_y(i, by):
    y = (i // CORES % SIDE_Y + by) % SIDE_Y
    return i // LINE * LINE + y * CORES + i % CORES


def ring_gather(x, axis, up, down, count):
    below, above = [], []
    for _ in range(count // 2 - 1):
        below.append(lax.ppermute(below[-1] if below else x, axis, up))
        above.append(lax.ppermute(above[-1] if above else x, axis, down))
    half = x.shape[0] // 2
    far = [lax.ppermute(below[-1][:half], axis, up), lax.ppermute(above[-1][half:], axis, down)]
    return below, above, far


def ring_streams(low, high, axis, up, down, count):
    streams = {
        (True, False): [low],
        (False, True): [high],
        (True, True): [high],
        (False, False): [low],
    }
    for hop in range(count // 2):
        for (is_up, is_high), held in streams.items():
            if hop < count // 2 - 1 or is_up != is_high:
                held.append(lax.ppermute(held[-1], axis, up if is_up else down))
    blocks = [(low, high)]
    for is_up in (True, False):
        blocks += [(streams[is_up, False][n], streams[is_up, True][n]) for n in range(1, count // 2)]
    blocks.append((streams[True, False][count // 2], streams[False, True][count // 2]))
    return blocks


def project_kernel(
    place_ref, gain_ref, cos_ref, sin_ref, wq_hbm, wk_hbm, wv_hbm, *refs
):
    x_refs, (q_ref, keep_ref, send_ref, normed_ref, w_ref, sem) = refs[: 2 * SIDE_Z], refs[2 * SIDE_Z :]
    copies = [
        pltpu.make_async_copy(hbm, w_ref.at[:, pl.ds(at, hbm.shape[1])], sem.at[i])
        for i, (hbm, at) in enumerate(((wk_hbm, 0), (wv_hbm, HEAD_SIZE), (wq_hbm, 2 * HEAD_SIZE)))
    ]
    for copy in copies:
        copy.start()
    z, core = place_ref[0], place_ref[1]
    rows, width = normed_ref.shape[0], x_refs[0].shape[1]
    quarter = rows // QUARTERS
    heads = q_ref.shape[1] // quarter
    for s in range(QUARTERS):
        here = slice(s * quarter, (s + 1) * quarter)
        span = slice(s % 2 * quarter, (s % 2 + 1) * quarter)
        views = [(k, x_refs[2 * n + s // 2], span) for n, k in enumerate(STEPS)]
        squares = jnp.zeros((quarter, HEAD_SIZE), jnp.float32)
        for _, ref, span in views:
            x = ref[span, :].astype(jnp.float32)
            for lane in range(0, width, HEAD_SIZE):
                piece = x[:, lane : lane + HEAD_SIZE]
                squares = squares + piece * piece
        inverse = lax.rsqrt(jnp.sum(squares, axis=1, keepdims=True) / MODEL_WIDTH + EPSILON)
        for k, ref, span in views:
            columns = pl.ds(pl.multiple_of(((z - k) & (SIDE_Z - 1)) * width, width), width)
            x = ref[span, :].astype(jnp.float32)
            normed_ref[here, columns] = (x * inverse * gain_ref[:, columns]).astype(jnp.bfloat16)

    def turned(head, here):
        return (head * cos_ref[here, :] + pltpu.roll(head, HEAD_SIZE // 2, 1) * sin_ref[here, :]).astype(jnp.bfloat16)

    for copy in copies:
        copy.wait()
    normed = normed_ref[...]
    pair = jnp.dot(normed, w_ref[:, : 2 * HEAD_SIZE], preferred_element_type=jnp.float32)
    for s in range(QUARTERS):
        here = slice(s * quarter, (s + 1) * quarter)
        keys = turned(pair[here, :HEAD_SIZE], here)
        values = pair[here, HEAD_SIZE:].T.astype(jnp.bfloat16)
        keep_ref[here, :] = jnp.where(core == 0, keys, values)
        send_ref[here, :] = jnp.where(core == 0, values, keys)
    for h in range(0, heads, 2):
        pair = jnp.dot(normed, w_ref[:, (h + 2) * HEAD_SIZE : (h + 4) * HEAD_SIZE], preferred_element_type=jnp.float32)
        for n in range(2):
            for s in range(QUARTERS):
                here = slice(s * quarter, (s + 1) * quarter)
                head = pair[here, n * HEAD_SIZE : (n + 1) * HEAD_SIZE]
                q_ref[s, (h + n) * quarter : (h + n + 1) * quarter, :] = turned(head, here)


def project(place, gathered, gain, weights, cos, sin, heads):
    gathered = [half for block in gathered for half in block]
    rows, width = cos.shape[0], sum(w.shape[1] for w in weights)
    quarter = rows // QUARTERS
    block = jax.ShapeDtypeStruct((rows, HEAD_SIZE), jnp.bfloat16)
    return pl.pallas_call(
        project_kernel,
        in_specs=[SMEM] + [VMEM] * 3 + [ANYWHERE] * 3 + [VMEM] * len(gathered),
        out_specs=[VMEM] * 3,
        out_shape=[jax.ShapeDtypeStruct((QUARTERS, heads * quarter, HEAD_SIZE), jnp.bfloat16), block, block],
        scratch_shapes=[pltpu.VMEM((rows, MODEL_WIDTH), jnp.bfloat16)]
        + [pltpu.VMEM((MODEL_WIDTH, width), jnp.bfloat16), pltpu.SemaphoreType.DMA((3,))],
        compiler_params=pltpu.CompilerParams(vmem_limit_bytes=56 * MIB),
        cost_estimate=pl.CostEstimate(
            flops=2 * rows * MODEL_WIDTH * width,
            bytes_accessed=2 * (rows * MODEL_WIDTH + MODEL_WIDTH * width),
            transcendentals=0,
        ),
        name="norm_project",
    )(place, gain, cos, sin, *weights, *gathered)


def gray(d):
    return d ^ (d >> 1)


def attend_groups(groups, wait_rest, info_ref, first_ref, q_refs, out_refs, k_buf, v_buf, top_ref, total_ref, mix_ref):
    wide = info_ref[16]
    columns = q_refs[0].shape[0]
    tile = k_buf.shape[1] // (SIDE_X * CORES)
    rows = tile // QUARTERS
    heads = columns // rows
    factor = math.log2(math.e) / math.sqrt(HEAD_SIZE)
    x, y = wide // LINE, wide % LINE // CORES

    def load(j):
        dx, dy, core = (x - j // LINE) & 3, (y - j % LINE // CORES) & 3, j % CORES
        row = pl.multiple_of((gray(dx) * CORES + core) * tile, tile)
        keys = k_buf[gray(dy), pl.ds(row, tile), :]
        row = pl.multiple_of((gray(dy) * CORES + core) * tile, tile)
        values = [v_buf[gray(dx), pl.ds(row + s * HEAD_SIZE, HEAD_SIZE), :] for s in range(QUARTERS)]
        return keys, jnp.concatenate(values, axis=1)

    for g, q_ref, out_ref in zip(groups, q_refs, out_refs):
        low, own, base, late = (info_ref[4 * i + g] for i in range(4))
        top_ref[...] = jnp.full(top_ref.shape, NEGATIVE, jnp.float32)
        total_ref[...] = jnp.zeros(total_ref.shape, jnp.float32)
        mix_ref[...] = jnp.zeros(mix_ref.shape, jnp.float32)

        def step(j, tiles, masked):
            held = [load(j + n) for n in range(tiles)]
            keys = jnp.concatenate([k for k, _ in held], axis=0)
            values = jnp.concatenate([v for _, v in held], axis=1)
            scores = lax.dot_general(keys, q_ref[...], _NT, preferred_element_type=jnp.float32)
            if masked:
                key_pos = j * tile + lax.broadcasted_iota(jnp.int32, (tile * tiles, columns), 0)
                query_pos = base + (lax.broadcasted_iota(jnp.int32, (1, columns), 1) & (rows - 1))
                allowed = (key_pos >= first_ref[g]) & (key_pos <= query_pos)
                scores = jnp.where(allowed, scores, NEGATIVE)
            old = top_ref[...]
            new = jnp.maximum(old, jnp.max(scores, axis=0, keepdims=True))
            weights = jnp.exp2(scores * factor - new * factor)
            shrink = jnp.exp2((old - new) * factor)
            top_ref[...] = new
            total_ref[...] = total_ref[...] * shrink + jnp.sum(weights, axis=0, keepdims=True)
            mix_ref[...] = mix_ref[...] * shrink + jnp.dot(
                values, weights.astype(jnp.bfloat16), preferred_element_type=jnp.float32
            )

        step(own, 1, True)
        if g == groups[0]:
            wait_rest()
        clear = jnp.minimum((late + tile - 1) // tile, own)
        pairs = (own - clear) // 2
        lax.fori_loop(low, clear, lambda j, _: (step(j, 1, True), 0)[1], 0)
        lax.fori_loop(0, pairs, lambda n, _: (step(clear + 2 * n, 2, False), 0)[1], 0)

        @pl.when(clear + 2 * pairs < own)
        def _():
            step(own - 1, 1, False)

        mixed = mix_ref[...] / total_ref[...]
        for h in range(heads):
            out_ref[:, h * HEAD_SIZE : (h + 1) * HEAD_SIZE] = mixed[:, h * rows : (h + 1) * rows].T.astype(jnp.bfloat16)


def attend_kernel(groups, info_ref, first_ref, *refs):
    count = len(groups)
    q_refs, mine, other, refs = refs[:count], refs[count : count + 5], refs[count + 5 : count + 10], refs[count + 10 :]
    out_refs, (k_buf, v_buf, top_ref, total_ref, mix_ref, sem) = refs[:count], refs[count:]
    core = info_ref[16] & 1
    spans = [(0, 0), (1, 0), (2, 0), (3, 0), (3, mine[3].shape[0])]

    def copies(keys, values):
        return [
            pltpu.make_async_copy(ref, buf.at[step, pl.ds(row, ref.shape[0]), :], sem.at[i, n])
            for i, (refs, buf) in enumerate(((keys, k_buf), (values, v_buf)))
            for n, (ref, (step, row)) in enumerate(zip(refs, spans))
        ]

    @pl.when(core == 0)
    def _():
        started = copies(mine, other)
        for copy in (started[0], *started[5:], *started[1:5]):
            copy.start()

    @pl.when(core != 0)
    def _():
        started = copies(other, mine)
        for copy in (started[0], *started[5:], *started[1:5]):
            copy.start()

    waits = copies(mine, other)
    for copy in (waits[0], *waits[5:]):
        copy.wait()

    def wait_rest():
        for copy in waits[1:5]:
            copy.wait()

    attend_groups(groups, wait_rest, info_ref, first_ref, q_refs, out_refs, k_buf, v_buf, top_ref, total_ref, mix_ref)


def attend(groups, info, first, queries, held, heads, name):
    columns = queries[0].shape[0]
    tile = columns * QUARTERS // heads
    keys = SIDE_X * SIDE_Y * CORES * tile
    count = len(groups)
    return pl.pallas_call(
        functools.partial(attend_kernel, groups),
        in_specs=[SMEM] + [VMEM] * (1 + count) + [ANYWHERE] * len(held),
        out_specs=[VMEM] * count,
        out_shape=[jax.ShapeDtypeStruct((tile // QUARTERS, heads * HEAD_SIZE), jnp.bfloat16)] * count,
        scratch_shapes=[
            pltpu.VMEM((4, *held[0].shape), jnp.bfloat16),
            pltpu.VMEM((4, *held[0].shape), jnp.bfloat16),
            pltpu.VMEM((1, columns), jnp.float32),
            pltpu.VMEM((1, columns), jnp.float32),
            pltpu.VMEM((HEAD_SIZE, columns), jnp.float32),
            pltpu.SemaphoreType.DMA((2, 5)),
        ],
        compiler_params=pltpu.CompilerParams(vmem_limit_bytes=50 * MIB),
        cost_estimate=pl.CostEstimate(
            flops=4 * count * columns * HEAD_SIZE * keys // 2,
            bytes_accessed=2 * 2 * keys * HEAD_SIZE,
            transcendentals=count * columns * keys // 2,
        ),
        name=name,
    )(info, first, *queries, *held)


def product_kernel(aheads, place_ref, m0, m1, m2, m3, w_ref, *refs):
    outs, mixed_ref = iter(refs), refs[-1]
    z, x = place_ref[0], place_ref[2]
    quarter = m0.shape[0]
    for away, ref in zip(AWAY, (m0, m1, m2, m3)):
        row = ((x + away) & (QUARTERS - 1)) * quarter
        mixed_ref[pl.ds(pl.multiple_of(row, quarter), quarter), :] = ref[...]
    mixed = mixed_ref[...]
    width = w_ref.shape[1] // SIDE_Z
    half = mixed.shape[0] // 2
    for ahead in aheads:
        columns = pl.ds(pl.multiple_of(((z + ahead) & (SIDE_Z - 1)) * width, width), width)
        block = jnp.dot(mixed, w_ref[:, columns], preferred_element_type=jnp.float32).astype(jnp.bfloat16)
        next(outs)[...] = block[:half]
        next(outs)[...] = block[half:]


def product(aheads, place, pieces, w_out, name):
    rows, features = pieces[0].shape[0] * QUARTERS, pieces[0].shape[1]
    width = w_out.shape[1] // SIDE_Z
    block = lambda n: jax.ShapeDtypeStruct((n, width), jnp.bfloat16)
    sums = pl.pallas_call(
        functools.partial(product_kernel, aheads),
        in_specs=[SMEM] + [VMEM] * 5,
        out_specs=[VMEM] * 2 * len(aheads),
        out_shape=[block(rows // 2)] * 2 * len(aheads),
        scratch_shapes=[pltpu.VMEM((rows, features), jnp.bfloat16)],
        compiler_params=pltpu.CompilerParams(vmem_limit_bytes=16 * MIB),
        cost_estimate=pl.CostEstimate(
            flops=2 * rows * features * width * len(aheads),
            bytes_accessed=2 * (rows * features + (features + rows) * width * len(aheads)),
            transcendentals=0,
        ),
        name=name,
    )(place, *pieces, w_out)
    return {(ahead, part): sums[2 * n + part] for n, ahead in enumerate(aheads) for part in range(2)}


def add_rounded(a, *others):
    total = a.astype(jnp.float32)
    for b in others:
        total = total + b.astype(jnp.float32)
    return total.astype(jnp.bfloat16)


def ring_scatter(blocks, up, down):
    streams = {
        (1, 0): [4, 3, 2, 1],
        (-1, 1): [4, -3, -2, -1],
        (1, 1): [3, 2, 1],
        (-1, 0): [-3, -2, -1],
    }
    carried = {}
    for hop in range(4):
        for key, stops in streams.items():
            if hop < len(stops):
                block = blocks[stops[hop], key[1]]
                if key in carried:
                    block = add_rounded(block, carried[key])
                carried[key] = lax.ppermute(block, "narrow", up if key[0] > 0 else down)
    return jnp.concatenate([add_rounded(blocks[0, part], carried[1, part], carried[-1, part]) for part in range(2)])


def per_device(wide, narrow, tokens, norm_gain, w_query, key_weight, value_weight, w_out, doc_lengths):
    rows = tokens.shape[0]
    wide_index = lax.axis_index("wide")
    z = lax.axis_index("narrow")
    x, core = wide_index // LINE, wide_index % CORES
    heads = w_query.shape[1] // HEAD_SIZE
    quarter = rows // QUARTERS
    z_up = [(i, (i + 1) % narrow) for i in range(narrow)]
    z_down = [(b, a) for a, b in z_up]
    place = jnp.stack([z, core, x]).astype(jnp.int32)

    with jax.named_scope("gather_tokens"):
        gathered = ring_streams(tokens[: rows // 2], tokens[rows // 2 :], "narrow", z_up, z_down, narrow)
    with jax.named_scope("gather_gain"):
        gain = norm_gain.reshape(1, -1)
        for bit in (1, 2, 4):
            other = lax.ppermute(gain, "narrow", [(i, i ^ bit) for i in range(narrow)])
            gain = jnp.where(
                (z & bit) != 0, jnp.concatenate([other, gain], axis=1), jnp.concatenate([gain, other], axis=1)
            )

    with jax.named_scope("positions"):
        docs = doc_lengths.shape[0]
        earlier = jnp.arange(docs)[None, :] < jnp.arange(docs)[:, None]
        starts = jnp.sum(jnp.where(earlier, doc_lengths[None, :], 0), axis=1)

        def first_of(positions):
            return jnp.max(
                jnp.where(starts[None, :] <= positions[:, None], starts[None, :], 0), axis=1
            ).astype(jnp.int32)

        positions = wide_index * rows + jnp.arange(rows, dtype=jnp.int32)
        half = HEAD_SIZE // 2
        frequency = ROPE_BASE ** (-(jnp.arange(half, dtype=jnp.float32) * 2.0 / HEAD_SIZE))
        angles = (positions - first_of(positions)).astype(jnp.float32)[:, None] * frequency[None, :]
        cosine, sine = jnp.cos(angles), jnp.sin(angles)
        cos = jnp.concatenate([cosine, cosine], axis=1)
        sin = jnp.concatenate([-sine, sine], axis=1)

        blocks = (x - jnp.array(AWAY, jnp.int32)) % SIDE_X * LINE + wide_index % LINE
        bases = blocks * rows + x * quarter
        first = first_of((bases[:, None] + jnp.arange(quarter, dtype=jnp.int32)[None, :]).reshape(-1))
        first = first.reshape(len(AWAY), 1, quarter)
        info = jnp.concatenate(
            [first[:, 0, 0] // rows, blocks, bases, first[:, 0, -1], wide_index.reshape(1)]
        ).astype(jnp.int32)
        first = jnp.tile(first, (1, 1, heads))

    cos, sin, first, info, place = lax.optimization_barrier((cos, sin, first, info, place))
    q, keep, send = project(
        place, gathered, gain, (w_query, key_weight, value_weight), cos, sin, heads
    )

    def by_core(of_keys, of_values):
        up = [(i, (of_values if i % CORES else of_keys)(i, 1)) for i in range(wide)]
        return up, [(b, a) for a, b in up]

    swap = [(i, i ^ 1) for i in range(wide)]
    with jax.named_scope("gather_keys_values"):
        received = lax.ppermute(send, "wide", swap)
        base = jnp.where(
            core == 0, jnp.concatenate([keep, received], axis=0), jnp.concatenate([received, keep], axis=0)
        )
        up, down = by_core(shift_x, shift_y)
        far = [(i, dict(up)[dict(up)[i]]) for i in range(wide)]
        base = jnp.concatenate([base, *(lax.ppermute(base, "wide", pairs) for pairs in (up, down, far))], axis=0)
        below, above, far = ring_gather(base, "wide", *by_core(shift_y, shift_x), SIDE_X)
        mine = [base, *below, *above, *far]
        other = [lax.ppermute(block, "wide", swap) for block in mine]

    def along_x(away):
        return [(i, shift_x(i, away)) for i in range(wide)]

    with jax.named_scope("deal_queries"):
        queries = []
        for away in AWAY:
            piece = lax.dynamic_index_in_dim(q, (x + away) % SIDE_X, 0, keepdims=False)
            queries.append(lax.ppermute(piece, "wide", along_x(away)) if away else piece)

    mixed = attend((1, 2, 3), info, first, queries[1:], mine + other, heads, "attend_far")
    with jax.named_scope("deal_heads"):
        mixed = [lax.ppermute(piece, "wide", along_x(-away)) for away, piece in zip(AWAY[1:], mixed)]
    (own,) = attend((0,), info, first, queries[:1], mine + other, heads, "attend_own")

    sums = product((4, 3, -3), place, [own, *mixed], w_out, "output_product_first")
    sums |= product((2, -2, 1, -1, 0), place, [own, *mixed], w_out, "output_product_rest")
    with jax.named_scope("sum_heads"):
        return ring_scatter(sums, z_up, z_down)


def solution(mesh):
    in_specs = (
        P("wide", "narrow"),
        P("narrow"),
        P(None, "narrow"),
        P(None, "narrow"),
        P(None, "narrow"),
        P("narrow", None),
        P(),
    )
    return jax.shard_map(
        functools.partial(per_device, mesh.shape["wide"], mesh.shape["narrow"]),
        mesh=mesh,
        in_specs=in_specs,
        out_specs=P("wide", "narrow"),
        check_vma=False,
    )
```

```python
import functools
import math

import jax
import jax.numpy as jnp
from jax import lax
from jax.experimental import pallas as pl
from jax.experimental.pallas import tpu as pltpu
from jax.sharding import PartitionSpec as P

MODEL_WIDTH = 4096
HEAD_SIZE = 128
EPSILON = 1e-05
ROPE_BASE = 500000.0
NEGATIVE = -1e30
MIB = 1024 * 1024
SIDE_X, SIDE_Y, CORES, SIDE_Z = 4, 4, 2, 8
LINE = SIDE_Y * CORES
QUARTERS = SIDE_X
AWAY = (0, 1, 2, -1)
HEADER = 16
STEPS = (0, 1, 2, 3, -1, -2, -3, 4)

_NT = (((1,), (1,)), ((), ()))
VMEM = pl.BlockSpec(memory_space=pltpu.VMEM)
SMEM = pl.BlockSpec(memory_space=pltpu.SMEM)
ANYWHERE = pl.BlockSpec(memory_space=pl.ANY)


def shift_x(i, by):
    return (i // LINE + by) % SIDE_X * LINE + i % LINE


def shift_y(i, by):
    y = (i // CORES % SIDE_Y + by) % SIDE_Y
    return i // LINE * LINE + y * CORES + i % CORES


def ring_gather(x, axis, up, down, count):
    below, above = [], []
    for _ in range(count // 2 - 1):
        below.append(lax.ppermute(below[-1] if below else x, axis, up))
        above.append(lax.ppermute(above[-1] if above else x, axis, down))
    half = x.shape[0] // 2
    far = [lax.ppermute(below[-1][:half], axis, up), lax.ppermute(above[-1][half:], axis, down)]
    return below, above, far


def ring_streams(low, high, axis, up, down, count):
    streams = {
        (True, False): [low],
        (False, False): [low],
        (True, True): [high],
        (False, True): [high],
    }
    for hop in range(count // 2):
        for (is_up, is_high), held in streams.items():
            if hop < count // 2 - 1 or is_up != is_high:
                held.append(lax.ppermute(held[-1], axis, up if is_up else down))
    blocks = [(low, high)]
    for is_up in (True, False):
        blocks += [(streams[is_up, False][n], streams[is_up, True][n]) for n in range(1, count // 2)]
    blocks.append((streams[True, False][count // 2], streams[False, True][count // 2]))
    return blocks


def project_kernel(
    place_ref, cos_ref, sin_ref, wq_hbm, wk_hbm, wv_hbm, *refs
):
    x_refs, (q_ref, keep_ref, send_ref, normed_ref, w_ref, sem) = refs[: 2 * SIDE_Z], refs[2 * SIDE_Z :]
    copies = [
        pltpu.make_async_copy(hbm, w_ref.at[:, pl.ds(at, hbm.shape[1])], sem.at[i])
        for i, (hbm, at) in enumerate(((wk_hbm, 0), (wv_hbm, HEAD_SIZE), (wq_hbm, 2 * HEAD_SIZE)))
    ]
    for copy in copies:
        copy.start()
    z, core = place_ref[0], place_ref[1]
    rows, width = normed_ref.shape[0], x_refs[0].shape[1]
    quarter = rows // QUARTERS
    heads = q_ref.shape[1] // quarter
    gains = []
    for n in range(SIDE_Z):
        parts = x_refs[2 * n + 1][:HEADER, :].astype(jnp.float32)
        gains.append(parts[0:1] + (parts[1:2] + parts[2:3]))
    for s in range(QUARTERS):
        here = slice(s * quarter, (s + 1) * quarter)
        row = s % 2 * quarter + s // 2 * HEADER
        span = slice(row, row + quarter)
        views = [(k, x_refs[2 * n + s // 2], span) for n, k in enumerate(STEPS)]
        squares = jnp.zeros((quarter, HEAD_SIZE), jnp.float32)
        for _, ref, span in views:
            x = ref[span, :].astype(jnp.float32)
            for lane in range(0, width, HEAD_SIZE):
                piece = x[:, lane : lane + HEAD_SIZE]
                squares = squares + piece * piece
        inverse = lax.rsqrt(jnp.sum(squares, axis=1, keepdims=True) / MODEL_WIDTH + EPSILON)
        for (k, ref, span), gain in zip(views, gains):
            columns = pl.ds(pl.multiple_of(((z - k) & (SIDE_Z - 1)) * width, width), width)
            x = ref[span, :].astype(jnp.float32)
            normed_ref[here, columns] = (x * inverse * gain).astype(jnp.bfloat16)

    def turned(head, here):
        return (head * cos_ref[here, :] + pltpu.roll(head, HEAD_SIZE // 2, 1) * sin_ref[here, :]).astype(jnp.bfloat16)

    for copy in copies:
        copy.wait()
    normed = normed_ref[...]
    pair = jnp.dot(normed, w_ref[:, : 2 * HEAD_SIZE], preferred_element_type=jnp.float32)
    for s in range(QUARTERS):
        here = slice(s * quarter, (s + 1) * quarter)
        keys = turned(pair[here, :HEAD_SIZE], here)
        values = pair[here, HEAD_SIZE:].T.astype(jnp.bfloat16)
        keep_ref[here, :] = jnp.where(core == 0, keys, values)
        send_ref[here, :] = jnp.where(core == 0, values, keys)
    for h in range(0, heads, 2):
        pair = jnp.dot(normed, w_ref[:, (h + 2) * HEAD_SIZE : (h + 4) * HEAD_SIZE], preferred_element_type=jnp.float32)
        for n in range(2):
            for s in range(QUARTERS):
                here = slice(s * quarter, (s + 1) * quarter)
                head = pair[here, n * HEAD_SIZE : (n + 1) * HEAD_SIZE]
                q_ref[s, (h + n) * quarter : (h + n + 1) * quarter, :] = turned(head, here)


def project(place, gathered, weights, cos, sin, heads):
    gathered = [half for block in gathered for half in block]
    rows, width = cos.shape[0], sum(w.shape[1] for w in weights)
    quarter = rows // QUARTERS
    block = jax.ShapeDtypeStruct((rows, HEAD_SIZE), jnp.bfloat16)
    return pl.pallas_call(
        project_kernel,
        in_specs=[SMEM] + [VMEM] * 2 + [ANYWHERE] * 3 + [VMEM] * len(gathered),
        out_specs=[VMEM] * 3,
        out_shape=[jax.ShapeDtypeStruct((QUARTERS, heads * quarter, HEAD_SIZE), jnp.bfloat16), block, block],
        scratch_shapes=[pltpu.VMEM((rows, MODEL_WIDTH), jnp.bfloat16)]
        + [pltpu.VMEM((MODEL_WIDTH, width), jnp.bfloat16), pltpu.SemaphoreType.DMA((3,))],
        compiler_params=pltpu.CompilerParams(vmem_limit_bytes=56 * MIB),
        cost_estimate=pl.CostEstimate(
            flops=2 * rows * MODEL_WIDTH * width,
            bytes_accessed=2 * (rows * MODEL_WIDTH + MODEL_WIDTH * width),
            transcendentals=0,
        ),
        name="norm_project",
    )(place, cos, sin, *weights, *gathered)


def gray(d):
    return d ^ (d >> 1)


def attend_groups(groups, wait_rest, info_ref, first_ref, q_refs, out_refs, k_buf, v_buf, top_ref, total_ref, mix_ref):
    wide = info_ref[16]
    columns = q_refs[0].shape[0]
    tile = k_buf.shape[1] // (SIDE_X * CORES)
    rows = tile // QUARTERS
    heads = columns // rows
    factor = math.log2(math.e) / math.sqrt(HEAD_SIZE)
    x, y = wide // LINE, wide % LINE // CORES

    def load(j):
        dx, dy, core = (x - j // LINE) & 3, (y - j % LINE // CORES) & 3, j % CORES
        row = pl.multiple_of((gray(dx) * CORES + core) * tile, tile)
        keys = k_buf[gray(dy), pl.ds(row, tile), :]
        row = pl.multiple_of((gray(dy) * CORES + 1 - core) * tile, tile)
        values = [v_buf[gray(dx), pl.ds(row + s * HEAD_SIZE, HEAD_SIZE), :] for s in range(QUARTERS)]
        return keys, jnp.concatenate(values, axis=1)

    for g, q_ref, out_ref in zip(groups, q_refs, out_refs):
        low, own, base, late = (info_ref[4 * i + g] for i in range(4))
        top_ref[...] = jnp.full(top_ref.shape, NEGATIVE, jnp.float32)
        total_ref[...] = jnp.zeros(total_ref.shape, jnp.float32)
        mix_ref[...] = jnp.zeros(mix_ref.shape, jnp.float32)

        def step(j, tiles, masked):
            held = [load(j + n) for n in range(tiles)]
            keys = jnp.concatenate([k for k, _ in held], axis=0)
            values = jnp.concatenate([v for _, v in held], axis=1)
            scores = lax.dot_general(keys, q_ref[...], _NT, preferred_element_type=jnp.float32)
            if masked:
                key_pos = j * tile + lax.broadcasted_iota(jnp.int32, (tile * tiles, columns), 0)
                query_pos = base + (lax.broadcasted_iota(jnp.int32, (1, columns), 1) & (rows - 1))
                allowed = (key_pos >= first_ref[g]) & (key_pos <= query_pos)
                scores = jnp.where(allowed, scores, NEGATIVE)
            old = top_ref[...]
            new = jnp.maximum(old, jnp.max(scores, axis=0, keepdims=True))
            weights = jnp.exp2(scores * factor - new * factor)
            shrink = jnp.exp2((old - new) * factor)
            top_ref[...] = new
            total_ref[...] = total_ref[...] * shrink + jnp.sum(weights, axis=0, keepdims=True)
            mix_ref[...] = mix_ref[...] * shrink + jnp.dot(
                values, weights.astype(jnp.bfloat16), preferred_element_type=jnp.float32
            )

        step(own, 1, True)
        if g == groups[0]:
            wait_rest()
        clear = jnp.minimum((late + tile - 1) // tile, own)
        count = own - clear
        fours = count // 4
        lax.fori_loop(low, clear, lambda j, _: (step(j, 1, True), 0)[1], 0)
        lax.fori_loop(0, fours, lambda n, _: (step(clear + 4 * n, 4, False), 0)[1], 0)

        @pl.when(count % 4 >= 2)
        def _():
            step(clear + 4 * fours, 2, False)

        @pl.when(count % 2 == 1)
        def _():
            step(own - 1, 1, False)

        mixed = mix_ref[...] / total_ref[...]
        for h in range(heads):
            out_ref[:, h * HEAD_SIZE : (h + 1) * HEAD_SIZE] = mixed[:, h * rows : (h + 1) * rows].T.astype(jnp.bfloat16)


def attend_kernel(groups, info_ref, first_ref, *refs):
    count = len(groups)
    q_refs, mine, other, refs = refs[:count], refs[count : count + 5], refs[count + 5 : count + 10], refs[count + 10 :]
    out_refs, (k_buf, v_buf, top_ref, total_ref, mix_ref, sem) = refs[:count], refs[count:]
    core = info_ref[16] & 1
    spans = [(0, 0), (1, 0), (2, 0), (3, 0), (3, mine[3].shape[0])]

    def copies(keys, values):
        return [
            pltpu.make_async_copy(ref, buf.at[step, pl.ds(row, ref.shape[0]), :], sem.at[i, n])
            for i, (refs, buf) in enumerate(((keys, k_buf), (values, v_buf)))
            for n, (ref, (step, row)) in enumerate(zip(refs, spans))
        ]

    @pl.when(core == 0)
    def _():
        started = copies(mine, other)
        for copy in (started[0], *started[5:], *started[1:5]):
            copy.start()

    @pl.when(core != 0)
    def _():
        started = copies(other, mine)
        for copy in (started[0], *started[5:], *started[1:5]):
            copy.start()

    waits = copies(mine, other)
    for copy in (waits[0], *waits[5:]):
        copy.wait()

    def wait_rest():
        for copy in waits[1:5]:
            copy.wait()

    attend_groups(groups, wait_rest, info_ref, first_ref, q_refs, out_refs, k_buf, v_buf, top_ref, total_ref, mix_ref)


def attend(groups, info, first, queries, held, heads, name):
    columns = queries[0].shape[0]
    tile = columns * QUARTERS // heads
    keys = SIDE_X * SIDE_Y * CORES * tile
    count = len(groups)
    return pl.pallas_call(
        functools.partial(attend_kernel, groups),
        in_specs=[SMEM] + [VMEM] * (1 + count) + [ANYWHERE] * len(held),
        out_specs=[VMEM] * count,
        out_shape=[jax.ShapeDtypeStruct((tile // QUARTERS, heads * HEAD_SIZE), jnp.bfloat16)] * count,
        scratch_shapes=[
            pltpu.VMEM((4, *held[0].shape), jnp.bfloat16),
            pltpu.VMEM((4, *held[0].shape), jnp.bfloat16),
            pltpu.VMEM((1, columns), jnp.float32),
            pltpu.VMEM((1, columns), jnp.float32),
            pltpu.VMEM((HEAD_SIZE, columns), jnp.float32),
            pltpu.SemaphoreType.DMA((2, 5)),
        ],
        compiler_params=pltpu.CompilerParams(vmem_limit_bytes=50 * MIB),
        cost_estimate=pl.CostEstimate(
            flops=4 * count * columns * HEAD_SIZE * keys // 2,
            bytes_accessed=2 * 2 * keys * HEAD_SIZE,
            transcendentals=count * columns * keys // 2,
        ),
        name=name,
    )(info, first, *queries, *held)


def product_kernel(aheads, place_ref, m0, m1, m2, m3, w_ref, *refs):
    outs, mixed_ref = iter(refs), refs[-1]
    z, x = place_ref[0], place_ref[2]
    quarter = m0.shape[0]
    for away, ref in zip(AWAY, (m0, m1, m2, m3)):
        row = ((x + away) & (QUARTERS - 1)) * quarter
        mixed_ref[pl.ds(pl.multiple_of(row, quarter), quarter), :] = ref[...]
    mixed = mixed_ref[...]
    width = w_ref.shape[1] // SIDE_Z
    half = mixed.shape[0] // 2
    for ahead in aheads:
        columns = pl.ds(pl.multiple_of(((z + ahead) & (SIDE_Z - 1)) * width, width), width)
        block = jnp.dot(mixed, w_ref[:, columns], preferred_element_type=jnp.float32).astype(jnp.bfloat16)
        next(outs)[...] = block[:half]
        next(outs)[...] = block[half:]


def product(aheads, place, pieces, w_out, name):
    rows, features = pieces[0].shape[0] * QUARTERS, pieces[0].shape[1]
    width = w_out.shape[1] // SIDE_Z
    block = lambda n: jax.ShapeDtypeStruct((n, width), jnp.bfloat16)
    sums = pl.pallas_call(
        functools.partial(product_kernel, aheads),
        in_specs=[SMEM] + [VMEM] * 5,
        out_specs=[VMEM] * 2 * len(aheads),
        out_shape=[block(rows // 2)] * 2 * len(aheads),
        scratch_shapes=[pltpu.VMEM((rows, features), jnp.bfloat16)],
        compiler_params=pltpu.CompilerParams(vmem_limit_bytes=16 * MIB),
        cost_estimate=pl.CostEstimate(
            flops=2 * rows * features * width * len(aheads),
            bytes_accessed=2 * (rows * features + (features + rows) * width * len(aheads)),
            transcendentals=0,
        ),
        name=name,
    )(place, *pieces, w_out)
    return {(ahead, part): sums[2 * n + part] for n, ahead in enumerate(aheads) for part in range(2)}


def add_rounded(a, *others):
    total = a.astype(jnp.float32)
    for b in others:
        total = total + b.astype(jnp.float32)
    return total.astype(jnp.bfloat16)


def ring_scatter(blocks, up, down):
    streams = {
        (1, 0): [4, 3, 2, 1],
        (-1, 1): [4, -3, -2, -1],
        (1, 1): [3, 2, 1],
        (-1, 0): [-3, -2, -1],
    }
    carried = {}
    for hop in range(4):
        for key, stops in streams.items():
            if hop < len(stops):
                block = blocks[stops[hop], key[1]]
                if key in carried:
                    block = add_rounded(block, carried[key])
                carried[key] = lax.ppermute(block, "narrow", up if key[0] > 0 else down)
    return jnp.concatenate([add_rounded(blocks[0, part], carried[1, part], carried[-1, part]) for part in range(2)])


def per_device(wide, narrow, tokens, norm_gain, w_query, key_weight, value_weight, w_out, doc_lengths):
    rows = tokens.shape[0]
    wide_index = lax.axis_index("wide")
    z = lax.axis_index("narrow")
    x, core = wide_index // LINE, wide_index % CORES
    heads = w_query.shape[1] // HEAD_SIZE
    quarter = rows // QUARTERS
    z_up = [(i, (i + 1) % narrow) for i in range(narrow)]
    z_down = [(b, a) for a, b in z_up]
    place = jnp.stack([z, core, x]).astype(jnp.int32)

    with jax.named_scope("gather_tokens"):
        gain = norm_gain.reshape(1, -1)
        parts = []
        for _ in range(3):
            parts.append(lax.reduce_precision(gain, 8, 7))
            gain = gain - parts[-1]
        header = jnp.concatenate(parts + [jnp.zeros((HEADER - 3, gain.shape[1]), jnp.float32)], axis=0)
        high = jnp.concatenate([header.astype(jnp.bfloat16), tokens[rows // 2 :]], axis=0)
        gathered = ring_streams(tokens[: rows // 2], high, "narrow", z_up, z_down, narrow)

    with jax.named_scope("positions"):
        docs = doc_lengths.shape[0]
        earlier = jnp.arange(docs)[None, :] < jnp.arange(docs)[:, None]
        starts = jnp.sum(jnp.where(earlier, doc_lengths[None, :], 0), axis=1)

        def first_of(positions):
            return jnp.max(
                jnp.where(starts[None, :] <= positions[:, None], starts[None, :], 0), axis=1
            ).astype(jnp.int32)

        positions = wide_index * rows + jnp.arange(rows, dtype=jnp.int32)
        half = HEAD_SIZE // 2
        frequency = ROPE_BASE ** (-(jnp.arange(half, dtype=jnp.float32) * 2.0 / HEAD_SIZE))
        angles = (positions - first_of(positions)).astype(jnp.float32)[:, None] * frequency[None, :]
        cosine, sine = jnp.cos(angles), jnp.sin(angles)
        cos = jnp.concatenate([cosine, cosine], axis=1)
        sin = jnp.concatenate([-sine, sine], axis=1)

        blocks = (x - jnp.array(AWAY, jnp.int32)) % SIDE_X * LINE + wide_index % LINE
        bases = blocks * rows + x * quarter
        first = first_of((bases[:, None] + jnp.arange(quarter, dtype=jnp.int32)[None, :]).reshape(-1))
        first = first.reshape(len(AWAY), 1, quarter)
        info = jnp.concatenate(
            [first[:, 0, 0] // rows, blocks, bases, first[:, 0, -1], wide_index.reshape(1)]
        ).astype(jnp.int32)
        first = jnp.tile(first, (1, 1, heads))

    cos, sin, first, info, place = lax.optimization_barrier((cos, sin, first, info, place))
    q, keep, send = project(
        place, gathered, (w_query, key_weight, value_weight), cos, sin, heads
    )

    def by_core(of_keys, of_values):
        up = [(i, (of_values if i % CORES else of_keys)(i, 1)) for i in range(wide)]
        return up, [(b, a) for a, b in up]

    swap = [(i, i ^ 1) for i in range(wide)]
    with jax.named_scope("gather_keys_values"):
        received = lax.ppermute(send, "wide", swap)
        base = jnp.concatenate([keep, received], axis=0)
        up, down = by_core(shift_x, shift_y)
        far = [(i, dict(up)[dict(up)[i]]) for i in range(wide)]
        base = jnp.concatenate([base, *(lax.ppermute(base, "wide", pairs) for pairs in (up, down, far))], axis=0)
        below, above, far = ring_gather(base, "wide", *by_core(shift_y, shift_x), SIDE_X)
        mine = [base, *below, *above, *far]
        other = [lax.ppermute(block, "wide", swap) for block in mine]

    def along_x(away):
        return [(i, shift_x(i, away)) for i in range(wide)]

    with jax.named_scope("deal_queries"):
        queries = []
        for away in AWAY:
            piece = lax.dynamic_index_in_dim(q, (x + away) % SIDE_X, 0, keepdims=False)
            queries.append(lax.ppermute(piece, "wide", along_x(away)) if away else piece)

    mixed = attend((1, 2, 3), info, first, queries[1:], mine + other, heads, "attend_far")
    with jax.named_scope("deal_heads"):
        mixed = [lax.ppermute(piece, "wide", along_x(-away)) for away, piece in zip(AWAY[1:], mixed)]
    (own,) = attend((0,), info, first, queries[:1], mine + other, heads, "attend_own")

    sums = product((4, 3, -3), place, [own, *mixed], w_out, "output_product_first")
    sums |= product((2, -2, 1, -1, 0), place, [own, *mixed], w_out, "output_product_rest")
    with jax.named_scope("sum_heads"):
        return ring_scatter(sums, z_up, z_down)


def solution(mesh):
    in_specs = (
        P("wide", "narrow"),
        P("narrow"),
        P(None, "narrow"),
        P(None, "narrow"),
        P(None, "narrow"),
        P("narrow", None),
        P(),
    )
    return jax.shard_map(
        functools.partial(per_device, mesh.shape["wide"], mesh.shape["narrow"]),
        mesh=mesh,
        in_specs=in_specs,
        out_specs=P("wide", "narrow"),
        check_vma=False,
    )
```

```python
import functools
import math

import jax
import jax.numpy as jnp
from jax import lax
from jax.experimental import pallas as pl
from jax.experimental.pallas import tpu as pltpu
from jax.sharding import PartitionSpec as P

MODEL_WIDTH = 4096
HEAD_SIZE = 128
EPSILON = 1e-05
ROPE_BASE = 500000.0
NEGATIVE = -1e30
MIB = 1024 * 1024
SIDE_X, SIDE_Y, CORES, SIDE_Z = 4, 4, 2, 8
LINE = SIDE_Y * CORES
QUARTERS = SIDE_X
AWAY = (0, 1, 2, -1)
HEADER = 16
STEPS = (0, 1, 2, 3, -1, -2, -3, 4)

_NT = (((1,), (1,)), ((), ()))
VMEM = pl.BlockSpec(memory_space=pltpu.VMEM)
SMEM = pl.BlockSpec(memory_space=pltpu.SMEM)
ANYWHERE = pl.BlockSpec(memory_space=pl.ANY)


def shift_x(i, by):
    return (i // LINE + by) % SIDE_X * LINE + i % LINE


def shift_y(i, by):
    y = (i // CORES % SIDE_Y + by) % SIDE_Y
    return i // LINE * LINE + y * CORES + i % CORES


def ring_gather(x, axis, up, down, count):
    below, above = [], []
    for _ in range(count // 2 - 1):
        below.append(lax.ppermute(below[-1] if below else x, axis, up))
        above.append(lax.ppermute(above[-1] if above else x, axis, down))
    half = x.shape[0] // 2
    far = [lax.ppermute(below[-1][:half], axis, up), lax.ppermute(above[-1][half:], axis, down)]
    return below, above, far


def ring_streams(low, high, axis, up, down, count):
    streams = {
        (True, False): [low],
        (False, False): [low],
        (True, True): [high],
        (False, True): [high],
    }
    for hop in range(count // 2):
        for (is_up, is_high), held in streams.items():
            if hop < count // 2 - 1 or is_up != is_high:
                held.append(lax.ppermute(held[-1], axis, up if is_up else down))
    blocks = [(low, high)]
    for is_up in (True, False):
        blocks += [(streams[is_up, False][n], streams[is_up, True][n]) for n in range(1, count // 2)]
    blocks.append((streams[True, False][count // 2], streams[False, True][count // 2]))
    return blocks


def project_kernel(
    place_ref, cos_ref, sin_ref, wq_hbm, wk_hbm, wv_hbm, *refs
):
    x_refs, (q_ref, keep_ref, send_ref, normed_ref, w_ref, sem) = refs[: 2 * SIDE_Z], refs[2 * SIDE_Z :]
    copies = [
        pltpu.make_async_copy(hbm, w_ref.at[:, pl.ds(at, hbm.shape[1])], sem.at[i])
        for i, (hbm, at) in enumerate(((wk_hbm, 0), (wv_hbm, HEAD_SIZE), (wq_hbm, 2 * HEAD_SIZE)))
    ]
    for copy in copies:
        copy.start()
    z, core = place_ref[0], place_ref[1]
    rows, width = normed_ref.shape[0], x_refs[0].shape[1]
    quarter = rows // QUARTERS
    heads = q_ref.shape[1] // quarter
    gains = []
    for n in range(SIDE_Z):
        parts = x_refs[2 * n + 1][:HEADER, :].astype(jnp.float32)
        gains.append(parts[0:1] + (parts[1:2] + parts[2:3]))
    for s in range(QUARTERS):
        here = slice(s * quarter, (s + 1) * quarter)
        row = s % 2 * quarter + s // 2 * HEADER
        span = slice(row, row + quarter)
        views = [(k, x_refs[2 * n + s // 2], span) for n, k in enumerate(STEPS)]
        squares = jnp.zeros((quarter, HEAD_SIZE), jnp.float32)
        for _, ref, span in views:
            x = ref[span, :].astype(jnp.float32)
            for lane in range(0, width, HEAD_SIZE):
                piece = x[:, lane : lane + HEAD_SIZE]
                squares = squares + piece * piece
        inverse = lax.rsqrt(jnp.sum(squares, axis=1, keepdims=True) / MODEL_WIDTH + EPSILON)
        for (k, ref, span), gain in zip(views, gains):
            columns = pl.ds(pl.multiple_of(((z - k) & (SIDE_Z - 1)) * width, width), width)
            x = ref[span, :].astype(jnp.float32)
            normed_ref[here, columns] = (x * inverse * gain).astype(jnp.bfloat16)

    def turned(head, here):
        return (head * cos_ref[here, :] + pltpu.roll(head, HEAD_SIZE // 2, 1) * sin_ref[here, :]).astype(jnp.bfloat16)

    for copy in copies:
        copy.wait()
    normed = normed_ref[...]
    pair = jnp.dot(normed, w_ref[:, : 2 * HEAD_SIZE], preferred_element_type=jnp.float32)
    for s in range(QUARTERS):
        here = slice(s * quarter, (s + 1) * quarter)
        keys = turned(pair[here, :HEAD_SIZE], here)
        values = pair[here, HEAD_SIZE:].T.astype(jnp.bfloat16)
        keep_ref[here, :] = jnp.where(core == 0, keys, values)
        send_ref[here, :] = jnp.where(core == 0, values, keys)
    for h in range(0, heads, 2):
        pair = jnp.dot(normed, w_ref[:, (h + 2) * HEAD_SIZE : (h + 4) * HEAD_SIZE], preferred_element_type=jnp.float32)
        for n in range(2):
            for s in range(QUARTERS):
                here = slice(s * quarter, (s + 1) * quarter)
                head = pair[here, n * HEAD_SIZE : (n + 1) * HEAD_SIZE]
                q_ref[s, (h + n) * quarter : (h + n + 1) * quarter, :] = turned(head, here)


def project(place, gathered, weights, cos, sin, heads):
    gathered = [half for block in gathered for half in block]
    rows, width = cos.shape[0], sum(w.shape[1] for w in weights)
    quarter = rows // QUARTERS
    block = jax.ShapeDtypeStruct((rows, HEAD_SIZE), jnp.bfloat16)
    return pl.pallas_call(
        project_kernel,
        in_specs=[SMEM] + [VMEM] * 2 + [ANYWHERE] * 3 + [VMEM] * len(gathered),
        out_specs=[VMEM] * 3,
        out_shape=[jax.ShapeDtypeStruct((QUARTERS, heads * quarter, HEAD_SIZE), jnp.bfloat16), block, block],
        scratch_shapes=[pltpu.VMEM((rows, MODEL_WIDTH), jnp.bfloat16)]
        + [pltpu.VMEM((MODEL_WIDTH, width), jnp.bfloat16), pltpu.SemaphoreType.DMA((3,))],
        compiler_params=pltpu.CompilerParams(vmem_limit_bytes=56 * MIB),
        cost_estimate=pl.CostEstimate(
            flops=2 * rows * MODEL_WIDTH * width,
            bytes_accessed=2 * (rows * MODEL_WIDTH + MODEL_WIDTH * width),
            transcendentals=0,
        ),
        name="norm_project",
    )(place, cos, sin, *weights, *gathered)


def gray(d):
    return d ^ (d >> 1)


def attend_groups(groups, wait_rest, info_ref, first_ref, q_refs, out_refs, k_buf, v_buf, top_ref, total_ref, mix_ref):
    wide = info_ref[16]
    columns = q_refs[0].shape[0]
    tile = k_buf.shape[1] // (SIDE_X * CORES)
    rows = tile // QUARTERS
    heads = columns // rows
    factor = math.log2(math.e) / math.sqrt(HEAD_SIZE)
    x, y = wide // LINE, wide % LINE // CORES

    def load(j):
        dx, dy, core = (x - j // LINE) & 3, (y - j % LINE // CORES) & 3, j % CORES
        row = pl.multiple_of((gray(dx) * CORES + core) * tile, tile)
        keys = k_buf[gray(dy), pl.ds(row, tile), :]
        row = pl.multiple_of((gray(dy) * CORES + 1 - core) * tile, tile)
        values = [v_buf[gray(dx), pl.ds(row + s * HEAD_SIZE, HEAD_SIZE), :] for s in range(QUARTERS)]
        return keys, jnp.concatenate(values, axis=1)

    for g, q_ref, out_ref in zip(groups, q_refs, out_refs):
        low, own, base, late = (info_ref[4 * i + g] for i in range(4))
        top_ref[...] = jnp.full(top_ref.shape, NEGATIVE, jnp.float32)
        total_ref[...] = jnp.zeros(total_ref.shape, jnp.float32)
        mix_ref[...] = jnp.zeros(mix_ref.shape, jnp.float32)

        def step(j, tiles, masked):
            held = [load(j + n) for n in range(tiles)]
            keys = jnp.concatenate([k for k, _ in held], axis=0)
            values = jnp.concatenate([v for _, v in held], axis=1)
            scores = lax.dot_general(keys, q_ref[...], _NT, preferred_element_type=jnp.float32)
            if masked:
                key_pos = j * tile + lax.broadcasted_iota(jnp.int32, (tile * tiles, columns), 0)
                query_pos = base + (lax.broadcasted_iota(jnp.int32, (1, columns), 1) & (rows - 1))
                allowed = (key_pos >= first_ref[g]) & (key_pos <= query_pos)
                scores = jnp.where(allowed, scores, NEGATIVE)
            old = top_ref[...]
            new = jnp.maximum(old, jnp.max(scores, axis=0, keepdims=True))
            weights = jnp.exp2(scores * factor - new * factor)
            shrink = jnp.exp2((old - new) * factor)
            top_ref[...] = new
            total_ref[...] = total_ref[...] * shrink + jnp.sum(weights, axis=0, keepdims=True)
            mix_ref[...] = mix_ref[...] * shrink + jnp.dot(
                values, weights.astype(jnp.bfloat16), preferred_element_type=jnp.float32
            )

        step(own, 1, True)
        if g == groups[0]:
            wait_rest()
        clear = jnp.minimum((late + tile - 1) // tile, own)
        count = own - clear
        eights = count // 8
        lax.fori_loop(low, clear, lambda j, _: (step(j, 1, True), 0)[1], 0)
        lax.fori_loop(0, eights, lambda n, _: (step(clear + 8 * n, 8, False), 0)[1], 0)

        @pl.when(count % 8 >= 4)
        def _():
            step(clear + 8 * eights, 4, False)

        @pl.when(count % 4 >= 2)
        def _():
            step(clear + count // 4 * 4, 2, False)

        @pl.when(count % 2 == 1)
        def _():
            step(own - 1, 1, False)

        mixed = mix_ref[...] / total_ref[...]
        for h in range(heads):
            out_ref[:, h * HEAD_SIZE : (h + 1) * HEAD_SIZE] = mixed[:, h * rows : (h + 1) * rows].T.astype(jnp.bfloat16)


def attend_kernel(groups, info_ref, first_ref, *refs):
    count = len(groups)
    q_refs, mine, other, refs = refs[:count], refs[count : count + 5], refs[count + 5 : count + 10], refs[count + 10 :]
    out_refs, (k_buf, v_buf, top_ref, total_ref, mix_ref, sem) = refs[:count], refs[count:]
    core = info_ref[16] & 1
    spans = [(0, 0), (1, 0), (2, 0), (3, 0), (3, mine[3].shape[0])]

    def copies(keys, values):
        return [
            pltpu.make_async_copy(ref, buf.at[step, pl.ds(row, ref.shape[0]), :], sem.at[i, n])
            for i, (refs, buf) in enumerate(((keys, k_buf), (values, v_buf)))
            for n, (ref, (step, row)) in enumerate(zip(refs, spans))
        ]

    @pl.when(core == 0)
    def _():
        started = copies(mine, other)
        for copy in (started[0], *started[5:], *started[1:5]):
            copy.start()

    @pl.when(core != 0)
    def _():
        started = copies(other, mine)
        for copy in (started[0], *started[5:], *started[1:5]):
            copy.start()

    waits = copies(mine, other)
    for copy in (waits[0], *waits[5:]):
        copy.wait()

    def wait_rest():
        for copy in waits[1:5]:
            copy.wait()

    attend_groups(groups, wait_rest, info_ref, first_ref, q_refs, out_refs, k_buf, v_buf, top_ref, total_ref, mix_ref)


def attend(groups, info, first, queries, held, heads, name):
    columns = queries[0].shape[0]
    tile = columns * QUARTERS // heads
    keys = SIDE_X * SIDE_Y * CORES * tile
    count = len(groups)
    return pl.pallas_call(
        functools.partial(attend_kernel, groups),
        in_specs=[SMEM] + [VMEM] * (1 + count) + [ANYWHERE] * len(held),
        out_specs=[VMEM] * count,
        out_shape=[jax.ShapeDtypeStruct((tile // QUARTERS, heads * HEAD_SIZE), jnp.bfloat16)] * count,
        scratch_shapes=[
            pltpu.VMEM((4, *held[0].shape), jnp.bfloat16),
            pltpu.VMEM((4, *held[0].shape), jnp.bfloat16),
            pltpu.VMEM((1, columns), jnp.float32),
            pltpu.VMEM((1, columns), jnp.float32),
            pltpu.VMEM((HEAD_SIZE, columns), jnp.float32),
            pltpu.SemaphoreType.DMA((2, 5)),
        ],
        compiler_params=pltpu.CompilerParams(vmem_limit_bytes=50 * MIB),
        cost_estimate=pl.CostEstimate(
            flops=4 * count * columns * HEAD_SIZE * keys // 2,
            bytes_accessed=2 * 2 * keys * HEAD_SIZE,
            transcendentals=count * columns * keys // 2,
        ),
        name=name,
    )(info, first, *queries, *held)


def product_kernel(aheads, place_ref, m0, m1, m2, m3, w_ref, *refs):
    outs, mixed_ref = iter(refs), refs[-1]
    z, x = place_ref[0], place_ref[2]
    quarter = m0.shape[0]
    for away, ref in zip(AWAY, (m0, m1, m2, m3)):
        row = ((x + away) & (QUARTERS - 1)) * quarter
        mixed_ref[pl.ds(pl.multiple_of(row, quarter), quarter), :] = ref[...]
    mixed = mixed_ref[...]
    width = w_ref.shape[1] // SIDE_Z
    half = mixed.shape[0] // 2
    for ahead in aheads:
        columns = pl.ds(pl.multiple_of(((z + ahead) & (SIDE_Z - 1)) * width, width), width)
        block = jnp.dot(mixed, w_ref[:, columns], preferred_element_type=jnp.float32).astype(jnp.bfloat16)
        next(outs)[...] = block[:half]
        next(outs)[...] = block[half:]


def product(aheads, place, pieces, w_out, name):
    rows, features = pieces[0].shape[0] * QUARTERS, pieces[0].shape[1]
    width = w_out.shape[1] // SIDE_Z
    block = lambda n: jax.ShapeDtypeStruct((n, width), jnp.bfloat16)
    sums = pl.pallas_call(
        functools.partial(product_kernel, aheads),
        in_specs=[SMEM] + [VMEM] * 5,
        out_specs=[VMEM] * 2 * len(aheads),
        out_shape=[block(rows // 2)] * 2 * len(aheads),
        scratch_shapes=[pltpu.VMEM((rows, features), jnp.bfloat16)],
        compiler_params=pltpu.CompilerParams(vmem_limit_bytes=16 * MIB),
        cost_estimate=pl.CostEstimate(
            flops=2 * rows * features * width * len(aheads),
            bytes_accessed=2 * (rows * features + (features + rows) * width * len(aheads)),
            transcendentals=0,
        ),
        name=name,
    )(place, *pieces, w_out)
    return {(ahead, part): sums[2 * n + part] for n, ahead in enumerate(aheads) for part in range(2)}


def add_rounded(a, *others):
    total = a.astype(jnp.float32)
    for b in others:
        total = total + b.astype(jnp.float32)
    return total.astype(jnp.bfloat16)


def ring_scatter(blocks, up, down):
    streams = {
        (1, 0): [4, 3, 2, 1],
        (-1, 1): [4, -3, -2, -1],
        (1, 1): [3, 2, 1],
        (-1, 0): [-3, -2, -1],
    }
    carried = {}
    for hop in range(4):
        for key, stops in streams.items():
            if hop < len(stops):
                block = blocks[stops[hop], key[1]]
                if key in carried:
                    block = add_rounded(block, carried[key])
                carried[key] = lax.ppermute(block, "narrow", up if key[0] > 0 else down)
    return jnp.concatenate([add_rounded(blocks[0, part], carried[1, part], carried[-1, part]) for part in range(2)])


def per_device(wide, narrow, tokens, norm_gain, w_query, key_weight, value_weight, w_out, doc_lengths):
    rows = tokens.shape[0]
    wide_index = lax.axis_index("wide")
    z = lax.axis_index("narrow")
    x, core = wide_index // LINE, wide_index % CORES
    heads = w_query.shape[1] // HEAD_SIZE
    quarter = rows // QUARTERS
    z_up = [(i, (i + 1) % narrow) for i in range(narrow)]
    z_down = [(b, a) for a, b in z_up]
    place = jnp.stack([z, core, x]).astype(jnp.int32)

    with jax.named_scope("gather_tokens"):
        gain = norm_gain.reshape(1, -1)
        parts = []
        for _ in range(3):
            parts.append(lax.reduce_precision(gain, 8, 7))
            gain = gain - parts[-1]
        header = jnp.concatenate(parts + [jnp.zeros((HEADER - 3, gain.shape[1]), jnp.float32)], axis=0)
        high = jnp.concatenate([header.astype(jnp.bfloat16), tokens[rows // 2 :]], axis=0)
        gathered = ring_streams(tokens[: rows // 2], high, "narrow", z_up, z_down, narrow)

    with jax.named_scope("positions"):
        docs = doc_lengths.shape[0]
        earlier = jnp.arange(docs)[None, :] < jnp.arange(docs)[:, None]
        starts = jnp.sum(jnp.where(earlier, doc_lengths[None, :], 0), axis=1)

        def first_of(positions):
            return jnp.max(
                jnp.where(starts[None, :] <= positions[:, None], starts[None, :], 0), axis=1
            ).astype(jnp.int32)

        positions = wide_index * rows + jnp.arange(rows, dtype=jnp.int32)
        half = HEAD_SIZE // 2
        frequency = ROPE_BASE ** (-(jnp.arange(half, dtype=jnp.float32) * 2.0 / HEAD_SIZE))
        angles = (positions - first_of(positions)).astype(jnp.float32)[:, None] * frequency[None, :]
        cosine, sine = jnp.cos(angles), jnp.sin(angles)
        cos = jnp.concatenate([cosine, cosine], axis=1)
        sin = jnp.concatenate([-sine, sine], axis=1)

        blocks = (x - jnp.array(AWAY, jnp.int32)) % SIDE_X * LINE + wide_index % LINE
        bases = blocks * rows + x * quarter
        first = first_of((bases[:, None] + jnp.arange(quarter, dtype=jnp.int32)[None, :]).reshape(-1))
        first = first.reshape(len(AWAY), 1, quarter)
        info = jnp.concatenate(
            [first[:, 0, 0] // rows, blocks, bases, first[:, 0, -1], wide_index.reshape(1)]
        ).astype(jnp.int32)
        first = jnp.tile(first, (1, 1, heads))

    cos, sin, first, info, place = lax.optimization_barrier((cos, sin, first, info, place))
    q, keep, send = project(
        place, gathered, (w_query, key_weight, value_weight), cos, sin, heads
    )

    def by_core(of_keys, of_values):
        up = [(i, (of_values if i % CORES else of_keys)(i, 1)) for i in range(wide)]
        return up, [(b, a) for a, b in up]

    swap = [(i, i ^ 1) for i in range(wide)]
    with jax.named_scope("gather_keys_values"):
        received = lax.ppermute(send, "wide", swap)
        base = jnp.concatenate([keep, received], axis=0)
        up, down = by_core(shift_x, shift_y)
        far = [(i, dict(up)[dict(up)[i]]) for i in range(wide)]
        base = jnp.concatenate([base, *(lax.ppermute(base, "wide", pairs) for pairs in (up, down, far))], axis=0)
        below, above, far = ring_gather(base, "wide", *by_core(shift_y, shift_x), SIDE_X)
        mine = [base, *below, *above, *far]
        other = [lax.ppermute(block, "wide", swap) for block in mine]

    def along_x(away):
        return [(i, shift_x(i, away)) for i in range(wide)]

    with jax.named_scope("deal_queries"):
        queries = []
        for away in AWAY:
            piece = lax.dynamic_index_in_dim(q, (x + away) % SIDE_X, 0, keepdims=False)
            queries.append(lax.ppermute(piece, "wide", along_x(away)) if away else piece)

    mixed = attend((1, 2, 3), info, first, queries[1:], mine + other, heads, "attend_far")
    with jax.named_scope("deal_heads"):
        mixed = [lax.ppermute(piece, "wide", along_x(-away)) for away, piece in zip(AWAY[1:], mixed)]
    (own,) = attend((0,), info, first, queries[:1], mine + other, heads, "attend_own")

    sums = product((4, 3, -3), place, [own, *mixed], w_out, "output_product_first")
    sums |= product((2, -2, 1, -1, 0), place, [own, *mixed], w_out, "output_product_rest")
    with jax.named_scope("sum_heads"):
        return ring_scatter(sums, z_up, z_down)


def solution(mesh):
    in_specs = (
        P("wide", "narrow"),
        P("narrow"),
        P(None, "narrow"),
        P(None, "narrow"),
        P(None, "narrow"),
        P("narrow", None),
        P(),
    )
    return jax.shard_map(
        functools.partial(per_device, mesh.shape["wide"], mesh.shape["narrow"]),
        mesh=mesh,
        in_specs=in_specs,
        out_specs=P("wide", "narrow"),
        check_vma=False,
    )
```
